512 devices in a mesh: ctx: 32 (over x, z), inner: 16 (over y, core).
Axes of the slice: x: 4, y: 8, z: 8, core: 2. Of those that a mesh axis runs over, the one named last changes fastest.
Arguments:
- queries: bfloat16 [65536, 512], P(('ctx', 'inner')), may hold values from -8 to 8
- keys: bfloat16 [65536, 512], P(('ctx', 'inner')), may hold values from -6 to 6
- values: bfloat16 [65536, 512], P(('ctx', 'inner')), may hold values from -6 to 6
- w_proj: bfloat16 [8, 64, 256], replicated, may hold values from -1.5 to 1.5
- ln_gain: float32 [2, 64], replicated, may hold values from 0.1 to 1.9
- ln_bias: float32 [2, 64], replicated, may hold values from -3 to 3
- cotangent: bfloat16 [65536, 512], P(('ctx', 'inner')), may hold values from -6 to 6
Outputs:
- attended: bfloat16 [65536, 512], P(('ctx', 'inner'))
- grad_queries: bfloat16 [65536, 512], P(('ctx', 'inner'))
- grad_keys: bfloat16 [65536, 512], P(('ctx', 'inner'))
- grad_values: bfloat16 [65536, 512], P(('ctx', 'inner'))
- grad_proj: float32 [32, 8, 64, 256], P('ctx', None, None, 'inner')
- grad_norm: float32 [4, 64], replicated
The draws below stay inside these ranges and needn't reach their ends.
All inputs are finite; a program needn't handle non-finite values.
Results may differ from the reference program's by a relative error of at most 0.012.
Values may be sent and summed in bfloat16 or wider, within the bound.
A program may use at most 64 MiB of HBM per device.

```python
import math
import jax
import jax.numpy as jnp
from jax import lax

HEADS = 8
DH = 64
LANDMARKS = 256
WIN = 128
TOKENS = 65536
FEATURES = 512
N_CTX = 32


def draw_keys(key, part):
    result = jnp.clip(jax.random.normal(jax.random.fold_in(key, 11), (TOKENS, HEADS * DH), jnp.float32), -6.0, 6.0)
    return result.astype(jnp.bfloat16)


def draw_queries(key, part):
    result = jnp.clip(jax.random.normal(jax.random.fold_in(key, 23), (TOKENS, HEADS * DH), jnp.float32), -6.0, 6.0)
    return result.astype(jnp.bfloat16)


def draw_w_proj(key, part):
    result = jnp.clip(0.375 * jax.random.normal(jax.random.fold_in(key, 37), (HEADS, DH, LANDMARKS), jnp.float32), -1.5, 1.5)
    return result.astype(jnp.bfloat16)


def shard_levels(rng, dims, shards, low, high):
    factor_of, own = 1.0, jax.random.fold_in(rng, 6)
    for dim, parts in shards:
        draws = jnp.exp(jax.random.uniform(jax.random.fold_in(own, dim), (parts,), jnp.float32, low / len(shards), high / len(shards)))
        factor_of = factor_of * jnp.repeat(draws, dims[dim] // parts).reshape([-1 if axis == dim else 1 for axis in range(len(dims))])
    return factor_of


def scatter_about(stream_key, dims, deviation, limit, pieces=(), held_as=jnp.bfloat16):
    values = deviation * jax.random.normal(stream_key, dims, jnp.float32)
    if pieces:
        values = values * shard_levels(stream_key, dims, pieces, -0.22, 0.18)
    return jnp.clip(values, -limit, limit).astype(held_as)


def setup_inputs(seed: int = 0) -> dict:
    streams_of = jax.random.split(jax.random.key(seed), 8)
    queries = draw_queries(jax.random.fold_in(streams_of[7], 71), 0)
    keys = draw_keys(jax.random.fold_in(streams_of[7], 71), 0)
    values = scatter_about(streams_of[2], (TOKENS, FEATURES), 1.0, 6.0, ((0, 512),))
    w_proj = draw_w_proj(jax.random.fold_in(streams_of[7], 71), 0)
    ln_gain = jnp.clip(1.0 + 0.18 * jax.random.normal(streams_of[4], (2, DH), jnp.float32), 0.1, 1.9)
    ln_bias = scatter_about(streams_of[5], (2, DH), 0.5, 3.0, (), jnp.float32)
    cotangent = scatter_about(streams_of[6], (TOKENS, FEATURES), 1.0, 6.0, ((0, 512),))
    return dict(queries=queries, keys=keys, values=values, w_proj=w_proj, ln_gain=ln_gain, ln_bias=ln_bias, cotangent=cotangent)


def rounded(values_in):
    narrowed = lax.optimization_barrier(values_in.astype(jnp.bfloat16))
    return narrowed.astype(jnp.float32)

def normalise(landmark, gain_row, bias_row):
    average = lax.optimization_barrier(jnp.mean(landmark, axis=-1, keepdims=True))
    centred = landmark - average
    variance = lax.optimization_barrier(jnp.mean(centred * centred, axis=-1, keepdims=True))
    inverse = 1.0 / jnp.sqrt(variance + 1e-05)
    normed = centred * inverse
    return (normed, inverse, normed * gain_row + bias_row)

def norm_backward(grad_out, normed, inverse, gain_row):
    grad_normed = grad_out * gain_row
    first_mean = lax.optimization_barrier(jnp.mean(grad_normed, axis=-1, keepdims=True))
    second_mean = lax.optimization_barrier(jnp.mean(grad_normed * normed, axis=-1, keepdims=True))
    grad_in = inverse * (grad_normed - first_mean - normed * second_mean)
    return (grad_in, lax.optimization_barrier(jnp.sum(grad_out * normed, axis=(0, 1))), lax.optimization_barrier(jnp.sum(grad_out, axis=(0, 1))))

def reference(queries, keys, values, w_proj, ln_gain, ln_bias, cotangent):
    segments = TOKENS // WIN
    per_group = segments // N_CTX
    edge = 3 * WIN
    score_scale = 1.0 / math.sqrt(DH)
    query_seg = queries.reshape(segments, WIN, HEADS, DH)
    key_seg = keys.reshape(segments, WIN, HEADS, DH)
    value_seg = values.reshape(segments, WIN, HEADS, DH)
    grad_seg = cotangent.reshape(segments, WIN, HEADS, DH)
    w_full = w_proj.astype(jnp.float32)
    pad_spec = ((1, 1), (0, 0), (0, 0), (0, 0))
    key_pad = jnp.pad(key_seg, pad_spec)
    value_pad = jnp.pad(value_seg, pad_spec)
    query_pad = jnp.pad(query_seg, pad_spec)
    grad_pad = jnp.pad(grad_seg, pad_spec)

    def seg_logits(block):
        return jnp.einsum('thd,hdr->htr', block.astype(jnp.float32), w_full)

    def peak_step(carry, block):
        return (jnp.maximum(carry, lax.optimization_barrier(jnp.max(seg_logits(block), axis=1))), None)
    column_peak = lax.scan(peak_step, jnp.full((HEADS, LANDMARKS), -1e+30, jnp.float32), key_seg)[0]

    def total_step(carry, blocks):
        exponent = jnp.exp(seg_logits(blocks[0]) - column_peak[:, None, :])
        narrowed = rounded(exponent)
        key_part = jnp.einsum('htr,thd->hrd', narrowed, blocks[0].astype(jnp.float32))
        value_part = jnp.einsum('htr,thd->hrd', narrowed, blocks[1].astype(jnp.float32))
        return ((carry[0] + lax.optimization_barrier(jnp.sum(exponent, axis=1)), carry[1] + key_part, carry[2] + value_part), None)
    start = (jnp.zeros((HEADS, LANDMARKS), jnp.float32), jnp.zeros((HEADS, LANDMARKS, DH), jnp.float32), jnp.zeros((HEADS, LANDMARKS, DH), jnp.float32))
    sums = lax.scan(total_step, start, (key_seg, value_seg))[0]
    column_total = sums[0]
    mean_keys = sums[1] / column_total[..., None]
    mean_values = sums[2] / column_total[..., None]
    normed_keys, inverse_keys, land_keys = normalise(mean_keys, ln_gain[0], ln_bias[0])
    normed_values, inverse_values, land_values = normalise(mean_values, ln_gain[1], ln_bias[1])
    land_key_r = rounded(land_keys).transpose(1, 0, 2)
    land_value_r = rounded(land_values).transpose(1, 0, 2)

    def attend_step(carry, seg_index):
        query_block = query_seg[seg_index].astype(jnp.float32)
        grad_block = grad_seg[seg_index].astype(jnp.float32)
        window_keys = lax.dynamic_slice_in_dim(key_pad, seg_index, 3, 0).reshape(edge, HEADS, DH).astype(jnp.float32)
        window_values = lax.dynamic_slice_in_dim(value_pad, seg_index, 3, 0).reshape(edge, HEADS, DH).astype(jnp.float32)
        all_keys = jnp.concatenate([window_keys, land_key_r], axis=0)
        all_values = jnp.concatenate([window_values, land_value_r], axis=0)
        neighbour = seg_index - 1 + jnp.arange(edge, dtype=jnp.int32) // WIN
        usable = jnp.concatenate([(neighbour >= 0) & (neighbour < segments), jnp.ones((LANDMARKS,), dtype=bool)])
        scores = jnp.einsum('qhd,khd->hqk', query_block, all_keys) * score_scale
        scores = jnp.where(usable[None, None, :], scores, -1e+30)
        row_peak = lax.optimization_barrier(jnp.max(scores, axis=-1))
        log_total = row_peak + jnp.log(lax.optimization_barrier(jnp.sum(jnp.exp(scores - row_peak[..., None]), axis=-1)))
        probs = jnp.exp(scores - log_total[..., None])
        narrowed = rounded(probs)
        output = jnp.einsum('hqk,khd->qhd', narrowed, all_values)
        delta = jnp.einsum('qhd,qhd->hq', grad_block, output)
        grad_probs = jnp.einsum('qhd,khd->hqk', grad_block, all_values)
        grad_scores = rounded(probs * (grad_probs - delta[..., None]))
        grad_query = jnp.einsum('hqk,khd->qhd', grad_scores, all_keys) * score_scale
        land_key_grad = carry[0] + jnp.einsum('hqr,qhd->hrd', grad_scores[..., edge:], query_block) * score_scale
        land_value_grad = carry[1] + jnp.einsum('hqr,qhd->hrd', narrowed[..., edge:], grad_block)
        results = (output.astype(jnp.bfloat16), grad_query.astype(jnp.bfloat16), log_total, delta)
        return ((land_key_grad, land_value_grad), results)
    land_start = (jnp.zeros((HEADS, LANDMARKS, DH), jnp.float32), jnp.zeros((HEADS, LANDMARKS, DH), jnp.float32))
    land_grads, forward_rows = lax.scan(attend_step, land_start, jnp.arange(segments, dtype=jnp.int32))
    attended = forward_rows[0].reshape(TOKENS, FEATURES)
    grad_queries = forward_rows[1].reshape(TOKENS, FEATURES)
    lse_pad = jnp.pad(forward_rows[2], ((1, 1), (0, 0), (0, 0)))
    delta_pad = jnp.pad(forward_rows[3], ((1, 1), (0, 0), (0, 0)))
    grad_mean_keys, gain_key_grad, bias_key_grad = norm_backward(land_grads[0], normed_keys, inverse_keys, ln_gain[0])
    grad_mean_values, gain_value_grad, bias_value_grad = norm_backward(land_grads[1], normed_values, inverse_values, ln_gain[1])
    grad_norm = jnp.stack([gain_key_grad, bias_key_grad, gain_value_grad, bias_value_grad])
    grad_key_r = rounded(grad_mean_keys)
    grad_value_r = rounded(grad_mean_values)
    scaled_keys = rounded(grad_mean_keys / column_total[..., None])
    scaled_values = rounded(grad_mean_values / column_total[..., None])

    def weights_of(key_block):
        narrowed = rounded(jnp.exp(seg_logits(key_block) - column_peak[:, None, :]))
        return (narrowed, narrowed / column_total[:, None, :])

    def proj_grad(key_block, value_block):
        first = jnp.einsum('thd,hrd->htr', key_block.astype(jnp.float32), grad_key_r)
        return first + jnp.einsum('thd,hrd->htr', value_block.astype(jnp.float32), grad_value_r)

    def column_step(carry, blocks):
        weights = weights_of(blocks[0])[1]
        return (carry + lax.optimization_barrier(jnp.sum(weights * proj_grad(blocks[0], blocks[1]), axis=1)), None)
    column_sum = lax.scan(column_step, jnp.zeros((HEADS, LANDMARKS), jnp.float32), (key_seg, value_seg))[0]

    def key_step(carry, seg_index):
        key_block = key_seg[seg_index].astype(jnp.float32)
        value_block = value_seg[seg_index].astype(jnp.float32)
        narrowed, weights = weights_of(key_seg[seg_index])
        grad_logit = rounded(weights * (proj_grad(key_seg[seg_index], value_seg[seg_index]) - column_sum[:, None, :]))
        grad_key = jnp.einsum('htr,hrd->thd', narrowed, scaled_keys) + jnp.einsum('htr,hdr->thd', grad_logit, w_full)
        grad_value = jnp.einsum('htr,hrd->thd', narrowed, scaled_values)
        new_carry = carry + jnp.einsum('thd,htr->hdr', key_block, grad_logit)
        for offset in (0, 1, 2):
            source = seg_index + offset
            real_seg = source - 1
            usable = (real_seg >= 0) & (real_seg < segments)
            query_block = query_pad[source].astype(jnp.float32)
            grad_block = grad_pad[source].astype(jnp.float32)
            cross = jnp.einsum('qhd,khd->hqk', query_block, key_block) * score_scale
            probs = jnp.where(usable, jnp.exp(cross - lse_pad[source][..., None]), 0.0)
            grad_probs = jnp.einsum('qhd,khd->hqk', grad_block, value_block)
            grad_scores = rounded(probs * (grad_probs - delta_pad[source][..., None]))
            grad_key = grad_key + jnp.einsum('hqk,qhd->khd', grad_scores, query_block) * score_scale
            grad_value = grad_value + jnp.einsum('hqk,qhd->khd', rounded(probs), grad_block)
        return (new_carry, (grad_key.astype(jnp.bfloat16), grad_value.astype(jnp.bfloat16)))

    def group_step(group):
        indices = group * per_group + jnp.arange(per_group, dtype=jnp.int32)
        return lax.scan(key_step, jnp.zeros((HEADS, DH, LANDMARKS), jnp.float32), indices)
    grad_proj, key_rows = lax.map(group_step, jnp.arange(N_CTX, dtype=jnp.int32))
    grad_keys = key_rows[0].reshape(TOKENS, FEATURES)
    grad_values = key_rows[1].reshape(TOKENS, FEATURES)
    return (attended, grad_queries, grad_keys, grad_values, grad_proj, grad_norm)
```

```python
import functools
import types

import jax
import jax.numpy as jnp
from jax import lax
from jax.experimental import pallas as pl
from jax.experimental.pallas import tpu as pltpu
from jax.sharding import Mesh
from jax.sharding import PartitionSpec as P

AXES = ("x", "z", "y", "c")
WIN = 128
DH = 64
LANDMARKS = 256
F32 = jnp.float32
BF16 = jnp.bfloat16


def rcopy(src, dst, send, recv, device):
    return pltpu.make_async_remote_copy(
        src_ref=src,
        dst_ref=dst,
        send_sem=send,
        recv_sem=recv,
        device_id=device,
        device_id_type=pl.DeviceIdType.MESH,
    )


def mm(a, b):
    return lax.dot_general(a, b, (((1,), (0,)), ((), ())), preferred_element_type=F32)


def mm_t(a, b):
    return lax.dot_general(a, b, (((1,), (1,)), ((), ())), preferred_element_type=F32)


def left_half(shape):
    return lax.broadcasted_iota(jnp.int32, shape, 1) < DH


def half_mean(x):
    left = left_half(x.shape)
    low = jnp.sum(jnp.where(left, x, 0.0), axis=1, keepdims=True)
    high = jnp.sum(jnp.where(left, 0.0, x), axis=1, keepdims=True)
    return jnp.where(left, low, high) * (1.0 / DH)


def pack_heads(a_ref, b_ref, pair):
    cols = pl.ds(pair * WIN, WIN)
    a, b = a_ref[:, cols].astype(F32), b_ref[:, cols].astype(F32)
    left = left_half(a.shape)
    even = jnp.where(left, a, pltpu.roll(b, DH, 1)).astype(BF16)
    odd = jnp.where(left, pltpu.roll(a, DH, 1), b).astype(BF16)
    return even, odd


def unpack_heads(even, odd):
    even, odd = even.astype(F32), odd.astype(F32)
    left = left_half(even.shape)
    a = jnp.where(left, even, pltpu.roll(odd, DH, 1)).astype(BF16)
    b = jnp.where(left, pltpu.roll(even, DH, 1), odd).astype(BF16)
    return a, b


def as_row(col, base):
    shape = (col.shape[0], WIN)
    diag = lax.broadcasted_iota(jnp.int32, shape, 1) == lax.broadcasted_iota(jnp.int32, shape, 0) + base
    return jnp.sum(jnp.where(diag, col, 0.0), axis=0, keepdims=True)


def as_col(row, n, base):
    shape = (n, WIN)
    diag = lax.broadcasted_iota(jnp.int32, shape, 1) == lax.broadcasted_iota(jnp.int32, shape, 0) + base
    return jnp.sum(jnp.where(diag, row, 0.0), axis=1, keepdims=True)


def combine(parts):
    peak = functools.reduce(jnp.maximum, [log_weight for _, log_weight in parts])
    scaled = [(mean, jnp.exp(log_weight - peak)) for mean, log_weight in parts]
    total = functools.reduce(lambda a, b: a + b, [w for _, w in scaled])
    mean = functools.reduce(lambda a, b: a + b, [m * w for m, w in scaled])
    return mean / total, peak + jnp.log(total)


def kernel(dims, names, *refs):
    X, Z, Y, C = dims
    R = types.SimpleNamespace(**dict(zip(names, refs)))
    NS = Y
    G = 2 * X
    CH = LANDMARKS // G
    N = 2 * Y
    POS = X * Z * 2
    x, z, y, c = (lax.axis_index(a) for a in AXES)
    r = x * 2 + c
    n = y * 2 + c
    g = x * Z + z
    pos = g * 2 + c

    def inner_dev(m):
        return (x, z, m // 2, lax.rem(m, 2))

    def plane_dev(o):
        p = lax.rem(r + o, G)
        return (p // 2, z, y, lax.rem(p, 2))

    def z_dev(o):
        return (x, lax.rem(z + o, Z), y, c)

    def chain_dev(q):
        q = lax.rem(q + POS, POS)
        return (q // (2 * Z), lax.rem(q // 2, Z), y, lax.rem(q, 2))

    far = chain_dev(pos + 2 * c - 1)
    right_dev, left_dev = chain_dev(pos + 1), chain_dev(pos - 1)

    barrier = pltpu.get_barrier_semaphore()
    count = 0
    for o in range(1, N):
        pl.semaphore_signal(barrier, 1, device_id=inner_dev(lax.rem(n + o, N)), device_id_type=pl.DeviceIdType.MESH)
        count += 1
    for xo in range(1, X):
        for c2 in range(2):
            pl.semaphore_signal(
                barrier, 1, device_id=(lax.rem(x + xo, X), z, y, c2), device_id_type=pl.DeviceIdType.MESH
            )
            count += 1
    for o in range(1, Z):
        pl.semaphore_signal(barrier, 1, device_id=z_dev(o), device_id_type=pl.DeviceIdType.MESH)
        count += 1
    pl.semaphore_signal(barrier, 1, device_id=far, device_id_type=pl.DeviceIdType.MESH)
    count += 1

    for pair in range(Y // 2):
        R.kvm[2 * pair], R.kvm[2 * pair + 1] = pack_heads(R.k, R.v, pair)
    pl.semaphore_wait(barrier, count)

    half = Y // 2
    core_in = y // half
    slot_in = lax.rem(y, half) * 2 + c
    self_in = c == core_in

    def send_in(src, dst, base, send, recv):
        for o in range(Y):
            to = lax.rem(y + o, Y)
            remote = rcopy(src.at[to], dst.at[base + slot_in], send.at[o], recv.at[slot_in], (x, z, to, core_in))
            if o:
                remote.start()
            else:
                pl.when(jnp.logical_not(self_in))(remote.start)

                @pl.when(self_in)
                def _():
                    pltpu.make_async_copy(src.at[y], dst.at[base + slot_in], recv.at[slot_in]).start()

    def sent_in(src, dst, base, send, recv):
        for o in range(Y):
            to = lax.rem(y + o, Y)
            remote = rcopy(src.at[to], dst.at[base + slot_in], send.at[o], recv.at[slot_in], (x, z, to, core_in))
            if o:
                remote.wait_send()
            else:
                pl.when(jnp.logical_not(self_in))(remote.wait_send)

    def received(src, dst, base, send, recv, j):
        rcopy(src.at[0], dst.at[base + j], send.at[0], recv.at[j], (x, z, y, c)).wait_recv()

    kv_move = (R.kvm, R.kvx, 1, R.kv_s, R.kv_r)
    qg_move = (R.qgm, R.qg, 0, R.qg_s, R.qg_r)
    send_in(*kv_move)
    for pair in range(Y // 2):
        R.qgm[2 * pair], R.qgm[2 * pair + 1] = pack_heads(R.q, R.g, pair)
    send_in(*qg_move)

    w_pad = jnp.concatenate([R.w[y], jnp.zeros((DH, LANDMARKS), BF16)], axis=0)
    R.wp[...] = w_pad
    R.wt[...] = w_pad.astype(F32).T.astype(BF16)
    gain = jnp.concatenate([R.gain[0:1, :], R.gain[1:2, :]], axis=1)
    bias = jnp.concatenate([R.bias[0:1, :], R.bias[1:2, :]], axis=1)

    for j in range(NS):
        received(*kv_move, j)

    kv_own = R.kvx[1 : NS + 1].reshape(NS * WIN, WIN)
    logits = mm_t(R.wt[...], kv_own)
    peak = jnp.max(logits, axis=1, keepdims=True)
    expo = jnp.exp(logits - peak)
    total = jnp.sum(expo, axis=1, keepdims=True)
    means = mm(expo.astype(BF16), kv_own) / total
    log_weights = peak + jnp.log(total)
    for p in range(G):
        rows = slice(p * CH, (p + 1) * CH)
        R.s1[p, 0:CH] = means[rows]
        R.s1[p, CH : CH + 8] = jnp.broadcast_to(as_row(log_weights[rows], 0), (8, WIN))

    def plane(send, o):
        return lax.rem(r + o, G)

    def scatter_copies(src, dst, send, recv):
        return [
            rcopy(src.at[lax.rem(r + o, G)], dst.at[o - 1], send.at[o - 1], recv.at[o - 1], plane_dev(o))
            for o in range(1, G)
        ]

    def z_copies(src, dst, send, recv):
        return [rcopy(src, dst.at[o - 1], send.at[o - 1], recv.at[o - 1], z_dev(o)) for o in range(1, Z)]

    def gather_copies(buf, send, recv):
        return [
            rcopy(buf.at[r], buf.at[r], send.at[o - 1], recv.at[o - 1], plane_dev(o)) for o in range(1, G)
        ]

    pending = []

    def start(copies):
        for copy in copies:
            copy.start()
        pending.extend(copies)
        return copies

    def arrive(copies):
        for copy in copies:
            copy.wait_recv()

    scatter_1 = start(scatter_copies(R.s1, R.r1, R.s1_s, R.s1_r))

    halo = start(
        [
            rcopy(R.kvx.at[NS], R.kvx.at[0], R.h_s.at[0], R.h_r.at[0], right_dev),
            rcopy(R.kvx.at[1], R.kvx.at[NS + 1], R.h_s.at[1], R.h_r.at[1], left_dev),
        ]
    )

    def transpose_kv(s):
        R.kvt[:, s * WIN : (s + 1) * WIN] = R.kvx[s].astype(F32).T.astype(BF16)

    for s in range(1, NS + 1):
        transpose_kv(s)

    def part_of(ref, o):
        return (ref[o, 0:CH], as_col(ref[o, CH : CH + 1], CH, 0))

    arrive(scatter_1)
    mean, log_weight = combine([part_of(R.s1, r)] + [part_of(R.r1, o) for o in range(G - 1)])
    R.s2[0:CH] = mean
    R.s2[CH : CH + 8] = jnp.broadcast_to(as_row(log_weight, 0), (8, WIN))
    z_1 = start(z_copies(R.s2, R.r2, R.s2_s, R.s2_r))

    arrive(halo)
    transpose_kv(0)
    transpose_kv(NS + 1)

    def window_scores(s):
        received(*qg_move, s)
        qg = R.qg[s]
        left = left_half(qg.shape)
        zero = jnp.zeros_like(qg)
        R.rr[s, 0:WIN] = jnp.where(left, qg * jnp.asarray(0.125, BF16), zero)
        R.rr[s, WIN : 2 * WIN] = jnp.where(left, zero, qg)
        R.gt[s] = qg.astype(F32).T[DH:]
        kv = R.kvx[s : s + 3].reshape(3 * WIN, WIN)
        both = mm_t(kv, R.rr[s])
        scores = both[:, 0:WIN]
        if s == 0:
            rows = lax.broadcasted_iota(jnp.int32, (3 * WIN, 1), 0)
            scores = scores + jnp.where((rows < WIN) & (pos == 0), -1e30, 0.0)
        if s == NS - 1:
            rows = lax.broadcasted_iota(jnp.int32, (3 * WIN, 1), 0)
            scores = scores + jnp.where((rows >= 2 * WIN) & (pos == POS - 1), -1e30, 0.0)
        R.sw[s] = scores
        R.gpw[s] = both[:, WIN:]
        top = jnp.max(scores, axis=0, keepdims=True)
        weight = jnp.exp(scores - top)
        R.mw[s] = jnp.broadcast_to(top, (8, WIN))
        R.lw[s] = jnp.broadcast_to(jnp.sum(weight, axis=0, keepdims=True), (8, WIN))
        R.ow[s] = mm(R.kvt[:, s * WIN : (s + 3) * WIN], weight.astype(BF16))

    split = (NS + 1) // 2
    for s in range(split):
        window_scores(s)

    arrive(z_1)
    mean, log_weight = combine(
        [(mean, log_weight)] + [part_of(R.r2, o) for o in range(Z - 1)]
    )
    centred = mean - half_mean(mean)
    inverse = 1.0 / jnp.sqrt(half_mean(centred * centred) + 1e-05)
    normed = centred * inverse
    R.land[r] = (normed * gain + bias).astype(BF16)
    gather_1 = start(gather_copies(R.land, R.g1_s, R.g1_r))
    base = lax.rem(r * CH, WIN)
    R.lt[r] = jnp.broadcast_to(as_row(log_weight, base), (8, WIN))
    gather_l = start(gather_copies(R.lt, R.gl_s, R.gl_r))

    for s in range(split, NS):
        window_scores(s)

    arrive(gather_1)

    land = R.land[...].reshape(LANDMARKS, WIN)
    land_t = land.astype(F32).T.astype(BF16)
    R.landt[...] = land_t
    for s in range(NS):
        both = mm_t(land, R.rr[s])
        scores = both[:, 0:WIN]
        top_w = R.mw[s, 0:1]
        top = jnp.maximum(top_w, jnp.max(scores, axis=0, keepdims=True))
        weight = jnp.exp(scores - top)
        shrink = jnp.exp(top_w - top)
        total = R.lw[s, 0:1] * shrink + jnp.sum(weight, axis=0, keepdims=True)
        per = 1.0 / total
        probs = weight * per
        probs_b = probs.astype(BF16)
        out_t = R.ow[s] * (shrink * per) + mm(land_t, probs_b)
        delta = jnp.sum(out_t[DH:] * R.gt[s], axis=0, keepdims=True)
        grad = (probs * (both[:, WIN:] - delta)).astype(BF16)
        R.dp[:, 2 * s * WIN : (2 * s + 1) * WIN] = grad
        R.dp[:, (2 * s + 1) * WIN : (2 * s + 2) * WIN] = probs_b
        R.ow[s] = out_t
        R.mw[s] = jnp.broadcast_to(top + jnp.log(total), (8, WIN))
        R.lw[s] = jnp.broadcast_to(delta, (8, WIN))
    R.s3[...] = mm(R.dp[...], R.rr[...].reshape(2 * NS * WIN, WIN)).reshape(G, CH, WIN)
    scatter_2 = start(scatter_copies(R.s3, R.r3, R.s3_s, R.s3_r))

    R.dkv[...] = jnp.zeros_like(R.dkv)

    def out_copy(s):
        seg = c * NS + s
        return rcopy(R.om.at[s], R.oi.at[y], R.o_s.at[s], R.o_r.at[y], (x, z, seg // 2, lax.rem(seg, 2)))

    def is_own(s):
        return n == c * NS + s

    def send_out(s, src, dst, send, recv):
        seg = c * NS + s
        copy = rcopy(src.at[s], dst.at[y], send.at[s], recv.at[y], (x, z, seg // 2, lax.rem(seg, 2)))
        pl.when(jnp.logical_not(is_own(s)))(copy.start)

        @pl.when(is_own(s))
        def _():
            pltpu.make_async_copy(src.at[s], dst.at[y], recv.at[y]).start()

    def sent_out(s, src, dst, send, recv):
        seg = c * NS + s
        copy = rcopy(src.at[s], dst.at[y], send.at[s], recv.at[y], (x, z, seg // 2, lax.rem(seg, 2)))
        pl.when(jnp.logical_not(is_own(s)))(copy.wait_send)

    def window_grads(s):
        probs = jnp.exp(R.sw[s] - R.mw[s, 0:1])
        grad = (probs * (R.gpw[s] - R.lw[s, 0:1])).astype(BF16)
        both = jnp.concatenate([grad, probs.astype(BF16)], axis=1)
        part = mm(both, R.rr[s])
        for i in range(3):
            R.dkv[s + i] += part[i * WIN : (i + 1) * WIN]
        grad_q = mm(R.kvt[:, s * WIN : (s + 3) * WIN], grad) + mm(
            R.landt[...], R.dp[:, 2 * s * WIN : (2 * s + 1) * WIN]
        )
        rows = lax.broadcasted_iota(jnp.int32, (WIN, WIN), 0) < DH
        packed = jnp.where(rows, grad_q * 0.125, R.ow[s])
        R.om[s] = packed.T.astype(BF16)
        send_out(s, R.om, R.oi, R.o_s, R.o_r)

    for s in range(split):
        window_grads(s)
    arrive(scatter_2)
    land_grad = R.s3[r]
    for o in range(G - 1):
        land_grad = land_grad + R.r3[o]
    R.s4[...] = land_grad
    z_2 = start(z_copies(R.s4, R.r4, R.s4_s, R.s4_r))
    for s in range(split, NS):
        window_grads(s)
    back = start(
        [
            rcopy(R.dkv.at[NS + 1], R.dh.at[0], R.d_s.at[0], R.d_r.at[0], right_dev),
            rcopy(R.dkv.at[0], R.dh.at[1], R.d_s.at[1], R.d_r.at[1], left_dev),
        ]
    )
    arrive(z_2)
    for o in range(Z - 1):
        land_grad = land_grad + R.r4[o]
    scaled = land_grad * gain
    grad_mean = inverse * (scaled - half_mean(scaled) - normed * half_mean(scaled * normed))
    grad_mean_b = grad_mean.astype(BF16)
    R.gkv[r] = grad_mean_b
    gather_2 = start(gather_copies(R.gkv, R.g2_s, R.g2_r))
    column = jnp.sum(grad_mean_b.astype(F32) * mean, axis=1, keepdims=True)
    R.ct[r] = jnp.concatenate(
        [
            as_row(column, base),
            jnp.sum(land_grad * normed, axis=0, keepdims=True),
            jnp.sum(land_grad, axis=0, keepdims=True),
            jnp.zeros((5, WIN), F32),
        ],
        axis=0,
    )
    gather_c = start(gather_copies(R.ct, R.gc_s, R.gc_r))

    def row_of(ref):
        per = WIN // CH
        rows = []
        for first in range(0, G, per):
            rows.append(functools.reduce(lambda a, b: a + b, [ref[p, 0:1] for p in range(first, first + per)]))
        return jnp.concatenate(rows, axis=1)

    arrive(gather_l)
    log_row = row_of(R.lt)
    for s in range(NS):
        R.wgt[s] = jnp.exp(mm(R.kvx[s + 1], R.wp[...]) - log_row)
    arrive(back)
    R.dkv[1] += R.dh[0]
    R.dkv[NS] += R.dh[1]

    for h in range(Y):
        rcopy(R.om.at[0], R.oi.at[h], R.o_s.at[0], R.o_r.at[h], (x, z, y, c)).wait_recv()
    for pair in range(Y // 2):
        cols = slice(pair * WIN, (pair + 1) * WIN)
        R.gq_o[:, cols], R.att_o[:, cols] = unpack_heads(R.oi[2 * pair], R.oi[2 * pair + 1])

    arrive(gather_2)
    arrive(gather_c)
    column_row = row_of(R.ct)
    grads = R.gkv[...].reshape(LANDMARKS, WIN)
    stacked = jnp.concatenate([grads, R.wt[...]], axis=0)
    for s in range(NS):
        weight = R.wgt[s]
        grad = (weight * (mm_t(R.kvx[s + 1], grads) - column_row)).astype(BF16)
        R.dl[s] = grad
        both = jnp.concatenate([weight.astype(BF16), grad], axis=1)
        R.km[s] = (mm(both, stacked) + R.dkv[s + 1]).astype(BF16)
        send_out(s, R.km, R.ki, R.k_s, R.k_r)
    proj = mm(R.kvt[:, WIN : (NS + 1) * WIN], R.dl[...].reshape(NS * WIN, LANDMARKS)).T
    LN = LANDMARKS // N
    norm_tile = functools.reduce(lambda a, b: a + b, [R.ct[p] for p in range(G)])
    for m in range(N):
        R.pm[m, 0:LN] = proj[m * LN : (m + 1) * LN]
        R.pm[m, LN : LN + 8] = norm_tile
    proj_copies = start(
        [
            rcopy(R.pm.at[lax.rem(n + o, N)], R.pi.at[n], R.p_s.at[o - 1], R.p_r.at[o - 1], inner_dev(lax.rem(n + o, N)))
            for o in range(1, N)
        ]
    )
    R.pi[n] = R.pm[n]
    for h in range(Y):
        rcopy(R.km.at[0], R.ki.at[h], R.k_s.at[0], R.k_r.at[h], (x, z, y, c)).wait_recv()
    for pair in range(Y // 2):
        cols = slice(pair * WIN, (pair + 1) * WIN)
        R.gk_o[:, cols], R.gv_o[:, cols] = unpack_heads(R.ki[2 * pair], R.ki[2 * pair + 1])
    arrive(proj_copies)
    for h in range(Y):
        R.gp_o[h] = R.pi[2 * h, 0:LN] + R.pi[2 * h + 1, 0:LN]
    sums = functools.reduce(lambda a, b: a + b, [R.pi[2 * h, LN : LN + 8] for h in range(Y)])
    R.gn_o[0:1] = sums[1:2, 0:DH]
    R.gn_o[1:2] = sums[2:3, 0:DH]
    R.gn_o[2:3] = sums[1:2, DH:]
    R.gn_o[3:4] = sums[2:3, DH:]

    sent_in(*kv_move)
    sent_in(*qg_move)
    for s in range(NS):
        sent_out(s, R.om, R.oi, R.o_s, R.o_r)
        sent_out(s, R.km, R.ki, R.k_s, R.k_r)
    for copy in pending:
        copy.wait_send()


def layer(dims, q, k, v, w, gain, bias, g):
    X, Z, Y, C = dims
    NS, G, N = Y, 2 * X, 2 * Y
    CH, LN = LANDMARKS // G, LANDMARKS // N
    block = (WIN, WIN)
    dma = pltpu.SemaphoreType.DMA
    scratch = dict(
        kvm=((Y, *block), BF16),
        qgm=((Y, *block), BF16),
        kvx=((NS + 2, *block), BF16),
        qg=((NS, *block), BF16),
        wp=((WIN, LANDMARKS), BF16),
        wt=((LANDMARKS, WIN), BF16),
        s1=((G, CH + 8, WIN), F32),
        r1=((G - 1, CH + 8, WIN), F32),
        s2=((CH + 8, WIN), F32),
        r2=((Z - 1, CH + 8, WIN), F32),
        kvt=((WIN, (NS + 2) * WIN), BF16),
        rr=((NS, 2 * WIN, WIN), BF16),
        gt=((NS, DH, WIN), F32),
        sw=((NS, 3 * WIN, WIN), F32),
        gpw=((NS, 3 * WIN, WIN), F32),
        mw=((NS, 8, WIN), F32),
        lw=((NS, 8, WIN), F32),
        ow=((NS, *block), F32),
        land=((G, CH, WIN), BF16),
        lt=((G, 8, WIN), F32),
        landt=((WIN, LANDMARKS), BF16),
        dp=((LANDMARKS, 2 * NS * WIN), BF16),
        s3=((G, CH, WIN), F32),
        r3=((G - 1, CH, WIN), F32),
        s4=((CH, WIN), F32),
        r4=((Z - 1, CH, WIN), F32),
        dkv=((NS + 2, *block), F32),
        dh=((2, *block), F32),
        om=((NS, *block), BF16),
        oi=((Y, *block), BF16),
        gkv=((G, CH, WIN), BF16),
        ct=((G, 8, WIN), F32),
        wgt=((NS, WIN, LANDMARKS), F32),
        dl=((NS, WIN, LANDMARKS), BF16),
        km=((NS, *block), BF16),
        ki=((Y, *block), BF16),
        pm=((N, LN + 8, WIN), F32),
        pi=((N, LN + 8, WIN), F32),
    )
    counts = dict(
        kv=Y, qg=Y, h=2, s1=G - 1, s2=Z - 1, g1=G - 1, gl=G - 1, s3=G - 1, s4=Z - 1, g2=G - 1, gc=G - 1,
        d=2, o=Y, k=Y, p=N - 1,
    )
    sems = {f"{name}_{side}": dma((count,)) for name, count in counts.items() for side in "sr"}
    outs = dict(
        att_o=((WIN, Y * DH), BF16),
        gq_o=((WIN, Y * DH), BF16),
        gk_o=((WIN, Y * DH), BF16),
        gv_o=((WIN, Y * DH), BF16),
        gp_o=((Y, LN, WIN), F32),
        gn_o=((4, DH), F32),
    )
    names = ("q", "k", "v", "w", "gain", "bias", "g", *outs, *scratch, *sems)
    att, gq, gk, gv, gp, gn = pl.pallas_call(
        functools.partial(kernel, dims, names),
        out_shape=[jax.ShapeDtypeStruct(*o) for o in outs.values()],
        in_specs=[pl.BlockSpec(memory_space=pltpu.VMEM)] * 7,
        out_specs=[pl.BlockSpec(memory_space=pltpu.VMEM)] * len(outs),
        scratch_shapes=[pltpu.VMEM(*s) for s in scratch.values()] + list(sems.values()),
        compiler_params=pltpu.CompilerParams(
            collective_id=0, has_side_effects=True, vmem_limit_bytes=40 * 1024 * 1024
        ),
    )(q, k, v, w, gain, bias, g)
    return att, gq, gk, gv, gp[:, :, :DH].transpose(0, 2, 1)[None], gn


def build(devices):
    finer = Mesh(devices, AXES)
    tokens = P(AXES, None)
    return jax.shard_map(
        functools.partial(layer, devices.shape),
        mesh=finer,
        in_specs=(tokens, tokens, tokens, P(), P(), P(), tokens),
        out_specs=(tokens, tokens, tokens, tokens, P(("x", "z"), None, None, ("y", "c")), P()),
        check_vma=False,
    )


def solution(mesh):
    return build(mesh.devices.reshape(4, 8, 8, 2))
```

```python
import functools
import types

import jax
import jax.numpy as jnp
from jax import lax
from jax.experimental import pallas as pl
from jax.experimental.pallas import tpu as pltpu
from jax.sharding import Mesh
from jax.sharding import PartitionSpec as P

AXES = ("x", "z", "y", "c")
WIN = 128
DH = 64
LANDMARKS = 256
F32 = jnp.float32
BF16 = jnp.bfloat16


def rcopy(src, dst, send, recv, device):
    return pltpu.make_async_remote_copy(
        src_ref=src,
        dst_ref=dst,
        send_sem=send,
        recv_sem=recv,
        device_id=device,
        device_id_type=pl.DeviceIdType.MESH,
    )


def mm(a, b):
    return lax.dot_general(a, b, (((1,), (0,)), ((), ())), preferred_element_type=F32)


def mm_t(a, b):
    return lax.dot_general(a, b, (((1,), (1,)), ((), ())), preferred_element_type=F32)


def left_half(shape):
    return lax.broadcasted_iota(jnp.int32, shape, 1) < DH


def half_mean(x):
    left = left_half(x.shape)
    low = jnp.sum(jnp.where(left, x, 0.0), axis=1, keepdims=True)
    high = jnp.sum(jnp.where(left, 0.0, x), axis=1, keepdims=True)
    return jnp.where(left, low, high) * (1.0 / DH)


def pack_heads(a_ref, b_ref, pair):
    cols = pl.ds(pair * WIN, WIN)
    a, b = a_ref[:, cols].astype(F32), b_ref[:, cols].astype(F32)
    left = left_half(a.shape)
    even = jnp.where(left, a, pltpu.roll(b, DH, 1)).astype(BF16)
    odd = jnp.where(left, pltpu.roll(a, DH, 1), b).astype(BF16)
    return even, odd


def unpack_heads(even, odd):
    even, odd = even.astype(F32), odd.astype(F32)
    left = left_half(even.shape)
    a = jnp.where(left, even, pltpu.roll(odd, DH, 1)).astype(BF16)
    b = jnp.where(left, pltpu.roll(even, DH, 1), odd).astype(BF16)
    return a, b


def as_row(col, base):
    shape = (col.shape[0], WIN)
    diag = lax.broadcasted_iota(jnp.int32, shape, 1) == lax.broadcasted_iota(jnp.int32, shape, 0) + base
    return jnp.sum(jnp.where(diag, col, 0.0), axis=0, keepdims=True)


def as_col(row, n, base):
    shape = (n, WIN)
    diag = lax.broadcasted_iota(jnp.int32, shape, 1) == lax.broadcasted_iota(jnp.int32, shape, 0) + base
    return jnp.sum(jnp.where(diag, row, 0.0), axis=1, keepdims=True)


def combine(parts):
    peak = functools.reduce(jnp.maximum, [log_weight for _, log_weight in parts])
    scaled = [(mean, jnp.exp(log_weight - peak)) for mean, log_weight in parts]
    total = functools.reduce(lambda a, b: a + b, [w for _, w in scaled])
    mean = functools.reduce(lambda a, b: a + b, [m * w for m, w in scaled])
    return mean / total, peak + jnp.log(total)


def kernel(dims, names, *refs):
    X, Z, Y, C = dims
    R = types.SimpleNamespace(**dict(zip(names, refs)))
    NS = Y
    G = 2 * X
    CH = LANDMARKS // G
    N = 2 * Y
    POS = X * Z * 2
    x, z, y, c = (lax.axis_index(a) for a in AXES)
    r = x * 2 + c
    n = y * 2 + c
    g = x * Z + z
    pos = g * 2 + c

    def inner_dev(m):
        return (x, z, m // 2, lax.rem(m, 2))

    def plane_dev(o):
        p = lax.rem(r + o, G)
        return (p // 2, z, y, lax.rem(p, 2))

    def z_dev(o):
        return (x, lax.rem(z + o, Z), y, c)

    def chain_dev(q):
        q = lax.rem(q + POS, POS)
        return (q // (2 * Z), lax.rem(q // 2, Z), y, lax.rem(q, 2))

    far = chain_dev(pos + 2 * c - 1)
    right_dev, left_dev = chain_dev(pos + 1), chain_dev(pos - 1)

    stores = {}

    def store(*which):
        for name in which:
            stores[name] = pltpu.make_async_copy(
                getattr(R, name + "_b"), getattr(R, name + "_o"), R.out_s.at[len(stores)]
            )
            stores[name].start()

    loads = {}
    for i, (name, src) in enumerate(
        (("k", R.k_i), ("v", R.v_i), ("q", R.q_i), ("g", R.g_i), ("w", R.w_i.at[y]), ("gain", R.gain_i), ("bias", R.bias_i))
    ):
        loads[name] = pltpu.make_async_copy(src, getattr(R, name), R.in_s.at[i])
        loads[name].start()

    barrier = pltpu.get_barrier_semaphore()
    count = 0
    for o in range(1, N):
        pl.semaphore_signal(barrier, 1, device_id=inner_dev(lax.rem(n + o, N)), device_id_type=pl.DeviceIdType.MESH)
        count += 1
    for xo in range(1, X):
        for c2 in range(2):
            pl.semaphore_signal(
                barrier, 1, device_id=(lax.rem(x + xo, X), z, y, c2), device_id_type=pl.DeviceIdType.MESH
            )
            count += 1
    for o in range(1, Z):
        pl.semaphore_signal(barrier, 1, device_id=z_dev(o), device_id_type=pl.DeviceIdType.MESH)
        count += 1
    pl.semaphore_signal(barrier, 1, device_id=far, device_id_type=pl.DeviceIdType.MESH)
    count += 1

    loads["k"].wait()
    loads["v"].wait()
    for pair in range(Y // 2):
        R.kvm[2 * pair], R.kvm[2 * pair + 1] = pack_heads(R.k, R.v, pair)
    pl.semaphore_wait(barrier, count)

    unsent = []
    half = Y // 2
    core_in = y // half
    slot_in = lax.rem(y, half) * 2 + c
    self_in = c == core_in

    def send_in(src, dst, base, send, recv):
        for o in range(Y):
            to = lax.rem(y + o, Y)
            remote = rcopy(src.at[to], dst.at[base + slot_in], send.at[o], recv.at[slot_in], (x, z, to, core_in))
            if o:
                remote.start()
                unsent.append(remote.wait_send)
            else:
                pl.when(jnp.logical_not(self_in))(remote.start)
                unsent.append(functools.partial(pl.when(jnp.logical_not(self_in)), remote.wait_send))

                @pl.when(self_in)
                def _():
                    pltpu.make_async_copy(src.at[y], dst.at[base + slot_in], recv.at[slot_in]).start()

    def received(src, dst, base, send, recv, j):
        rcopy(src.at[0], dst.at[base + j], send.at[0], recv.at[j], (x, z, y, c)).wait_recv()

    kv_move = (R.kvm, R.kvx, 1, R.kv_s, R.kv_r)
    qg_move = (R.qgm, R.qg, 0, R.qg_s, R.qg_r)
    send_in(*kv_move)
    loads["q"].wait()
    loads["g"].wait()
    for pair in range(Y // 2):
        R.qgm[2 * pair], R.qgm[2 * pair + 1] = pack_heads(R.q, R.g, pair)
    send_in(*qg_move)

    for name in ("w", "gain", "bias"):
        loads[name].wait()
    w_pad = jnp.concatenate([R.w[...], jnp.zeros((DH, LANDMARKS), BF16)], axis=0)
    R.wp[...] = w_pad
    R.wt[...] = w_pad.astype(F32).T.astype(BF16)
    gain = jnp.concatenate([R.gain[0:1, :], R.gain[1:2, :]], axis=1)
    bias = jnp.concatenate([R.bias[0:1, :], R.bias[1:2, :]], axis=1)

    for j in range(NS):
        received(*kv_move, j)

    kv_own = R.kvx[1 : NS + 1].reshape(NS * WIN, WIN)
    logits = mm_t(R.wt[...], kv_own)
    peak = jnp.max(logits, axis=1, keepdims=True)
    expo = jnp.exp(logits - peak)
    total = jnp.sum(expo, axis=1, keepdims=True)
    means = mm(expo.astype(BF16), kv_own) / total
    log_weights = peak + jnp.log(total)
    for p in range(G):
        rows = slice(p * CH, (p + 1) * CH)
        R.s1[p, 0:CH] = means[rows]
        R.s1[p, CH : CH + 8] = jnp.broadcast_to(as_row(log_weights[rows], 0), (8, WIN))

    def scatter_copies(src, dst, send, recv):
        return [
            rcopy(src.at[lax.rem(r + o, G)], dst.at[o - 1], send.at[o - 1], recv.at[o - 1], plane_dev(o))
            for o in range(1, G)
        ]

    def z_copies(src, dst, send, recv):
        return [rcopy(src, dst.at[o - 1], send.at[o - 1], recv.at[o - 1], z_dev(o)) for o in range(1, Z)]

    def gather_copies(buf, send, recv):
        return [
            rcopy(buf.at[r], buf.at[r], send.at[o - 1], recv.at[o - 1], plane_dev(o)) for o in range(1, G)
        ]

    def start(copies):
        for copy in copies:
            copy.start()
            unsent.append(copy.wait_send)
        return copies

    def arrive(copies):
        for copy in copies:
            copy.wait_recv()

    scatter_1 = start(scatter_copies(R.s1, R.r1, R.s1_s, R.s1_r))

    halo = start(
        [
            rcopy(R.kvx.at[NS], R.kvx.at[0], R.h_s.at[0], R.h_r.at[0], right_dev),
            rcopy(R.kvx.at[1], R.kvx.at[NS + 1], R.h_s.at[1], R.h_r.at[1], left_dev),
        ]
    )

    def transpose_kv(s):
        R.kvt[:, s * WIN : (s + 1) * WIN] = R.kvx[s].astype(F32).T.astype(BF16)

    for s in range(1, NS + 1):
        transpose_kv(s)

    def part_of(ref, o):
        return (ref[o, 0:CH], as_col(ref[o, CH : CH + 1], CH, 0))

    arrive(scatter_1)
    mean, log_weight = combine([part_of(R.s1, r)] + [part_of(R.r1, o) for o in range(G - 1)])
    R.s2[0:CH] = mean
    R.s2[CH : CH + 8] = jnp.broadcast_to(as_row(log_weight, 0), (8, WIN))
    z_1 = start(z_copies(R.s2, R.r2, R.s2_s, R.s2_r))

    arrive(halo)
    transpose_kv(0)
    transpose_kv(NS + 1)

    def window_scores(segs):
        for s in segs:
            received(*qg_move, s)
        for s in segs:
            qg = R.qg[s]
            left = left_half(qg.shape)
            zero = jnp.zeros_like(qg)
            R.rr[s, 0:WIN] = jnp.where(left, qg * jnp.asarray(0.125, BF16), zero)
            R.rr[s, WIN : 2 * WIN] = jnp.where(left, zero, qg)
        for s in segs:
            R.gt[s] = R.qg[s].astype(F32).T[DH:]
        for s in segs:
            both = mm_t(R.kvx[s : s + 3].reshape(3 * WIN, WIN), R.rr[s])
            scores = both[:, 0:WIN]
            if s == 0:
                rows = lax.broadcasted_iota(jnp.int32, (3 * WIN, 1), 0)
                scores = scores + jnp.where((rows < WIN) & (pos == 0), -1e30, 0.0)
            if s == NS - 1:
                rows = lax.broadcasted_iota(jnp.int32, (3 * WIN, 1), 0)
                scores = scores + jnp.where((rows >= 2 * WIN) & (pos == POS - 1), -1e30, 0.0)
            R.sw[s] = scores
            R.gpw[s] = both[:, WIN:]
        tops = {s: jnp.max(R.sw[s], axis=0, keepdims=True) for s in segs}
        weights = {}
        for s in segs:
            weight = jnp.exp(R.sw[s] - tops[s])
            R.mw[s] = jnp.broadcast_to(tops[s], (8, WIN))
            R.lw[s] = jnp.broadcast_to(jnp.sum(weight, axis=0, keepdims=True), (8, WIN))
            weights[s] = weight.astype(BF16)
        for s in segs:
            R.ow[s] = mm(R.kvt[:, s * WIN : (s + 3) * WIN], weights[s])

    split = (NS + 1) // 2
    window_scores(range(split))

    arrive(z_1)
    mean, log_weight = combine(
        [(mean, log_weight)] + [part_of(R.r2, o) for o in range(Z - 1)]
    )
    centred = mean - half_mean(mean)
    inverse = 1.0 / jnp.sqrt(half_mean(centred * centred) + 1e-05)
    normed = centred * inverse
    R.land[r] = (normed * gain + bias).astype(BF16)
    gather_1 = start(gather_copies(R.land, R.g1_s, R.g1_r))
    base = lax.rem(r * CH, WIN)
    R.lt[r] = jnp.broadcast_to(as_row(log_weight, base), (8, WIN))
    gather_l = start(gather_copies(R.lt, R.gl_s, R.gl_r))

    window_scores(range(split, NS))

    arrive(gather_1)

    land = R.land[...].reshape(LANDMARKS, WIN)
    land_t = land.astype(F32).T.astype(BF16)
    R.landt[...] = land_t
    every = range(NS)
    both = [mm_t(land, R.rr[s]) for s in every]
    tops = [jnp.maximum(R.mw[s, 0:1], jnp.max(both[s][:, 0:WIN], axis=0, keepdims=True)) for s in every]
    weights = [jnp.exp(both[s][:, 0:WIN] - tops[s]) for s in every]
    shrinks = [jnp.exp(R.mw[s, 0:1] - tops[s]) for s in every]
    totals = [R.lw[s, 0:1] * shrinks[s] + jnp.sum(weights[s], axis=0, keepdims=True) for s in every]
    pers = [1.0 / t for t in totals]
    probs = [w * per for w, per in zip(weights, pers)]
    for s in every:
        R.dp[:, (2 * s + 1) * WIN : (2 * s + 2) * WIN] = probs[s].astype(BF16)
        R.mw[s] = jnp.broadcast_to(tops[s] + jnp.log(totals[s]), (8, WIN))
    for s in every:
        R.ow[s] = R.ow[s] * (shrinks[s] * pers[s]) + mm(land_t, R.dp[:, (2 * s + 1) * WIN : (2 * s + 2) * WIN])
    deltas = [jnp.sum(R.ow[s, DH:] * R.gt[s], axis=0, keepdims=True) for s in every]
    for s in every:
        R.dp[:, 2 * s * WIN : (2 * s + 1) * WIN] = (probs[s] * (both[s][:, WIN:] - deltas[s])).astype(BF16)
        R.lw[s] = jnp.broadcast_to(deltas[s], (8, WIN))
    R.s3[...] = mm(R.dp[...], R.rr[...].reshape(2 * NS * WIN, WIN)).reshape(G, CH, WIN)
    scatter_2 = start(scatter_copies(R.s3, R.r3, R.s3_s, R.s3_r))

    R.dkv[...] = jnp.zeros_like(R.dkv)

    def is_own(s):
        return n == c * NS + s

    def send_out(s, src, dst, send, recv):
        seg = c * NS + s
        copy = rcopy(src.at[s], dst.at[y], send.at[s], recv.at[y], (x, z, seg // 2, lax.rem(seg, 2)))
        pl.when(jnp.logical_not(is_own(s)))(copy.start)
        unsent.append(functools.partial(pl.when(jnp.logical_not(is_own(s))), copy.wait_send))

        @pl.when(is_own(s))
        def _():
            pltpu.make_async_copy(src.at[s], dst.at[y], recv.at[y]).start()

    def window_grads(segs):
        grads, probs_b = {}, {}
        for s in segs:
            probs = jnp.exp(R.sw[s] - R.mw[s, 0:1])
            grads[s] = (probs * (R.gpw[s] - R.lw[s, 0:1])).astype(BF16)
            probs_b[s] = probs.astype(BF16)
        for s in segs:
            part = mm(jnp.concatenate([grads[s], probs_b[s]], axis=1), R.rr[s])
            for i in range(3):
                R.dkv[s + i] += part[i * WIN : (i + 1) * WIN]
        rows = lax.broadcasted_iota(jnp.int32, (WIN, WIN), 0) < DH
        packed = []
        for s in segs:
            grad_q = mm(R.kvt[:, s * WIN : (s + 3) * WIN], grads[s]) + mm(
                R.landt[...], R.dp[:, 2 * s * WIN : (2 * s + 1) * WIN]
            )
            packed.append(jnp.where(rows, grad_q * 0.125, R.ow[s]))
        for s, block in zip(segs, packed):
            R.om[s] = block.T.astype(BF16)
        for s in segs:
            send_out(s, R.om, R.oi, R.o_s, R.o_r)

    window_grads(range(split))
    arrive(scatter_2)
    land_grad = R.s3[r]
    for o in range(G - 1):
        land_grad = land_grad + R.r3[o]
    R.s4[...] = land_grad
    z_2 = start(z_copies(R.s4, R.r4, R.s4_s, R.s4_r))
    window_grads(range(split, NS))
    back = start(
        [
            rcopy(R.dkv.at[NS + 1], R.dh.at[0], R.d_s.at[0], R.d_r.at[0], right_dev),
            rcopy(R.dkv.at[0], R.dh.at[1], R.d_s.at[1], R.d_r.at[1], left_dev),
        ]
    )
    arrive(z_2)
    for o in range(Z - 1):
        land_grad = land_grad + R.r4[o]
    scaled = land_grad * gain
    grad_mean = inverse * (scaled - half_mean(scaled) - normed * half_mean(scaled * normed))
    grad_mean_b = grad_mean.astype(BF16)
    R.gkv[r] = grad_mean_b
    gather_2 = start(gather_copies(R.gkv, R.g2_s, R.g2_r))
    column = jnp.sum(grad_mean_b.astype(F32) * mean, axis=1, keepdims=True)
    R.ct[r] = jnp.concatenate(
        [
            as_row(column, base),
            jnp.sum(land_grad * normed, axis=0, keepdims=True),
            jnp.sum(land_grad, axis=0, keepdims=True),
            jnp.zeros((5, WIN), F32),
        ],
        axis=0,
    )
    gather_c = start(gather_copies(R.ct, R.gc_s, R.gc_r))

    def row_of(ref):
        per = WIN // CH
        rows = []
        for first in range(0, G, per):
            rows.append(functools.reduce(lambda a, b: a + b, [ref[p, 0:1] for p in range(first, first + per)]))
        return jnp.concatenate(rows, axis=1)

    arrive(gather_l)
    log_row = row_of(R.lt)
    for s in range(NS):
        R.wgt[s] = jnp.exp(mm(R.kvx[s + 1], R.wp[...]) - log_row)
    arrive(back)
    R.dkv[1] += R.dh[0]
    R.dkv[NS] += R.dh[1]

    for h in range(Y):
        rcopy(R.om.at[0], R.oi.at[h], R.o_s.at[0], R.o_r.at[h], (x, z, y, c)).wait_recv()
    for pair in range(Y // 2):
        cols = slice(pair * WIN, (pair + 1) * WIN)
        R.gq_b[:, cols], R.att_b[:, cols] = unpack_heads(R.oi[2 * pair], R.oi[2 * pair + 1])
    store("gq", "att")

    arrive(gather_2)
    arrive(gather_c)
    column_row = row_of(R.ct)
    grads = R.gkv[...].reshape(LANDMARKS, WIN)
    stacked = jnp.concatenate([grads, R.wt[...]], axis=0)
    for s in every:
        R.dl[s] = (R.wgt[s] * (mm_t(R.kvx[s + 1], grads) - column_row)).astype(BF16)
    for first in range(0, NS, 4):
        segs = range(first, min(first + 4, NS))
        for s in segs:
            both = jnp.concatenate([R.wgt[s].astype(BF16), R.dl[s]], axis=1)
            R.km[s] = (mm(both, stacked) + R.dkv[s + 1]).astype(BF16)
        for s in segs:
            send_out(s, R.km, R.ki, R.k_s, R.k_r)
    proj = mm(R.kvt[:, WIN : (NS + 1) * WIN], R.dl[...].reshape(NS * WIN, LANDMARKS)).T
    LN = LANDMARKS // N
    norm_tile = functools.reduce(lambda a, b: a + b, [R.ct[p] for p in range(G)])
    for m in range(N):
        R.pm[m, 0:LN] = proj[m * LN : (m + 1) * LN]
        R.pm[m, LN : LN + 8] = norm_tile
    proj_copies = start(
        [
            rcopy(R.pm.at[lax.rem(n + o, N)], R.pi.at[n], R.p_s.at[o - 1], R.p_r.at[o - 1], inner_dev(lax.rem(n + o, N)))
            for o in range(1, N)
        ]
    )
    R.pi[n] = R.pm[n]
    for h in range(Y):
        rcopy(R.km.at[0], R.ki.at[h], R.k_s.at[0], R.k_r.at[h], (x, z, y, c)).wait_recv()
    for pair in range(Y // 2):
        cols = slice(pair * WIN, (pair + 1) * WIN)
        R.gk_b[:, cols], R.gv_b[:, cols] = unpack_heads(R.ki[2 * pair], R.ki[2 * pair + 1])
    store("gk", "gv")
    arrive(proj_copies)
    for h in range(Y):
        R.gp_b[h] = (R.pi[2 * h, 0:LN] + R.pi[2 * h + 1, 0:LN])[:, 0:DH]
    sums = functools.reduce(lambda a, b: a + b, [R.pi[2 * h, LN : LN + 8] for h in range(Y)])
    R.gn_b[0:1] = sums[1:2, 0:DH]
    R.gn_b[1:2] = sums[2:3, 0:DH]
    R.gn_b[2:3] = sums[1:2, DH:]
    R.gn_b[3:4] = sums[2:3, DH:]

    store("gp", "gn")
    for wait in unsent:
        wait()
    for copy in stores.values():
        copy.wait()


def store_kernel(*refs):
    count = len(refs) // 2
    copies = [pltpu.make_async_copy(refs[i], refs[count + i], refs[-1].at[i]) for i in range(count)]
    for copy in copies:
        copy.start()
    for copy in copies:
        copy.wait()


def layer(dims, q, k, v, w, gain, bias, g):
    X, Z, Y, C = dims
    NS, G, N = Y, 2 * X, 2 * Y
    CH, LN = LANDMARKS // G, LANDMARKS // N
    block = (WIN, WIN)
    dma = pltpu.SemaphoreType.DMA
    tokens = ((WIN, Y * DH), BF16)
    scratch = dict(
        q=tokens,
        k=tokens,
        v=tokens,
        g=tokens,
        w=((DH, LANDMARKS), BF16),
        gain=((2, DH), F32),
        bias=((2, DH), F32),
        kvm=((Y, *block), BF16),
        qgm=((Y, *block), BF16),
        kvx=((NS + 2, *block), BF16),
        qg=((NS, *block), BF16),
        wp=((WIN, LANDMARKS), BF16),
        wt=((LANDMARKS, WIN), BF16),
        s1=((G, CH + 8, WIN), F32),
        r1=((G - 1, CH + 8, WIN), F32),
        s2=((CH + 8, WIN), F32),
        r2=((Z - 1, CH + 8, WIN), F32),
        kvt=((WIN, (NS + 2) * WIN), BF16),
        rr=((NS, 2 * WIN, WIN), BF16),
        gt=((NS, DH, WIN), F32),
        sw=((NS, 3 * WIN, WIN), F32),
        gpw=((NS, 3 * WIN, WIN), F32),
        mw=((NS, 8, WIN), F32),
        lw=((NS, 8, WIN), F32),
        ow=((NS, *block), F32),
        land=((G, CH, WIN), BF16),
        lt=((G, 8, WIN), F32),
        landt=((WIN, LANDMARKS), BF16),
        dp=((LANDMARKS, 2 * NS * WIN), BF16),
        s3=((G, CH, WIN), F32),
        r3=((G - 1, CH, WIN), F32),
        s4=((CH, WIN), F32),
        r4=((Z - 1, CH, WIN), F32),
        dkv=((NS + 2, *block), F32),
        dh=((2, *block), F32),
        om=((NS, *block), BF16),
        oi=((Y, *block), BF16),
        gkv=((G, CH, WIN), BF16),
        ct=((G, 8, WIN), F32),
        wgt=((NS, WIN, LANDMARKS), F32),
        dl=((NS, WIN, LANDMARKS), BF16),
        km=((NS, *block), BF16),
        ki=((Y, *block), BF16),
        pm=((N, LN + 8, WIN), F32),
        pi=((N, LN + 8, WIN), F32),
    )
    counts = dict(
        kv=Y, qg=Y, h=2, s1=G - 1, s2=Z - 1, g1=G - 1, gl=G - 1, s3=G - 1, s4=Z - 1, g2=G - 1, gc=G - 1,
        d=2, o=Y, k=Y, p=N - 1,
    )
    sems = {f"{name}_{side}": dma((count,)) for name, count in counts.items() for side in "sr"}
    sems["in_s"] = dma((7,))
    outs = dict(
        att_o=tokens,
        gq_o=tokens,
        gk_o=tokens,
        gv_o=tokens,
        gp_o=((Y, LN, DH), F32),
        gn_o=((4, DH), F32),
    )
    scratch.update({name[:-2] + "_b": o for name, o in outs.items()})
    sems["out_s"] = dma((len(outs),))
    names = ("q_i", "k_i", "v_i", "w_i", "gain_i", "bias_i", "g_i", *outs, *scratch, *sems)
    results = pl.pallas_call(
        functools.partial(kernel, dims, names),
        out_shape=[jax.ShapeDtypeStruct(*o) for o in outs.values()],
        in_specs=[pl.BlockSpec(memory_space=pl.ANY)] * 7,
        out_specs=[pl.BlockSpec(memory_space=pl.ANY)] * len(outs),
        scratch_shapes=[pltpu.VMEM(*s) for s in scratch.values()] + list(sems.values()),
        compiler_params=pltpu.CompilerParams(
            collective_id=0, has_side_effects=True, vmem_limit_bytes=60 * 1024 * 1024
        ),
    )(q, k, v, w, gain, bias, g)
    att, gq, gk, gv, gp, gn = pl.pallas_call(
        store_kernel,
        out_shape=[jax.ShapeDtypeStruct(*o) for o in outs.values()],
        in_specs=[pl.BlockSpec(memory_space=pl.ANY)] * len(outs),
        out_specs=[pl.BlockSpec(memory_space=pl.ANY)] * len(outs),
        scratch_shapes=[dma((len(outs),))],
    )(*results)
    return att, gq, gk, gv, gp.transpose(0, 2, 1)[None], gn


def build(devices):
    finer = Mesh(devices, AXES)
    tokens = P(AXES, None)
    return jax.shard_map(
        functools.partial(layer, devices.shape),
        mesh=finer,
        in_specs=(tokens, tokens, tokens, P(), P(), P(), tokens),
        out_specs=(tokens, tokens, tokens, tokens, P(("x", "z"), None, None, ("y", "c")), P()),
        check_vma=False,
    )


def solution(mesh):
    return build(mesh.devices.reshape(4, 8, 8, 2))
```

```python
import functools
import types

import jax
import jax.numpy as jnp
from jax import lax
from jax.experimental import pallas as pl
from jax.experimental.pallas import tpu as pltpu
from jax.sharding import Mesh
from jax.sharding import PartitionSpec as P

AXES = ("x", "z", "y", "c")
WIN = 128
DH = 64
LANDMARKS = 256
F32 = jnp.float32
BF16 = jnp.bfloat16


def rcopy(src, dst, send, recv, device):
    return pltpu.make_async_remote_copy(
        src_ref=src,
        dst_ref=dst,
        send_sem=send,
        recv_sem=recv,
        device_id=device,
        device_id_type=pl.DeviceIdType.MESH,
    )


def mm(a, b):
    return lax.dot_general(a, b, (((1,), (0,)), ((), ())), preferred_element_type=F32)


def mm_t(a, b):
    return lax.dot_general(a, b, (((1,), (1,)), ((), ())), preferred_element_type=F32)


def far_first(size):
    return sorted(range(1, size), key=lambda o: -min(o, size - o))


def left_half(shape):
    return lax.broadcasted_iota(jnp.int32, shape, 1) < DH


def half_mean(x):
    left = left_half(x.shape)
    low = jnp.sum(jnp.where(left, x, 0.0), axis=1, keepdims=True)
    high = jnp.sum(jnp.where(left, 0.0, x), axis=1, keepdims=True)
    return jnp.where(left, low, high) * (1.0 / DH)


def pack_heads(a_ref, b_ref, pair):
    cols = pl.ds(pair * WIN, WIN)
    a, b = a_ref[:, cols].astype(F32), b_ref[:, cols].astype(F32)
    left = left_half(a.shape)
    even = jnp.where(left, a, pltpu.roll(b, DH, 1)).astype(BF16)
    odd = jnp.where(left, pltpu.roll(a, DH, 1), b).astype(BF16)
    return even, odd


def unpack_heads(even, odd):
    even, odd = even.astype(F32), odd.astype(F32)
    left = left_half(even.shape)
    a = jnp.where(left, even, pltpu.roll(odd, DH, 1)).astype(BF16)
    b = jnp.where(left, pltpu.roll(even, DH, 1), odd).astype(BF16)
    return a, b


def as_row(col, base):
    shape = (col.shape[0], WIN)
    diag = lax.broadcasted_iota(jnp.int32, shape, 1) == lax.broadcasted_iota(jnp.int32, shape, 0) + base
    return jnp.sum(jnp.where(diag, col, 0.0), axis=0, keepdims=True)


def as_col(row, n, base):
    shape = (n, WIN)
    diag = lax.broadcasted_iota(jnp.int32, shape, 1) == lax.broadcasted_iota(jnp.int32, shape, 0) + base
    return jnp.sum(jnp.where(diag, row, 0.0), axis=1, keepdims=True)


def combine(parts):
    peak = functools.reduce(jnp.maximum, [log_weight for _, log_weight in parts])
    scaled = [(mean, jnp.exp(log_weight - peak)) for mean, log_weight in parts]
    total = functools.reduce(lambda a, b: a + b, [w for _, w in scaled])
    mean = functools.reduce(lambda a, b: a + b, [m * w for m, w in scaled])
    return mean / total, peak + jnp.log(total)


def kernel(dims, names, *refs):
    X, Z, Y, C = dims
    R = types.SimpleNamespace(**dict(zip(names, refs)))
    NS = Y
    G = 2 * X
    CH = LANDMARKS // G
    N = 2 * Y
    POS = X * Z * 2
    x, z, y, c = (lax.axis_index(a) for a in AXES)
    r = x * 2 + c
    n = y * 2 + c
    g = x * Z + z
    pos = g * 2 + c

    def inner_dev(m):
        return (x, z, m // 2, lax.rem(m, 2))

    def plane_dev(o):
        p = lax.rem(r + o, G)
        return (p // 2, z, y, lax.rem(p, 2))

    def z_dev(o):
        return (x, lax.rem(z + o, Z), y, c)

    def chain_dev(q):
        q = lax.rem(q + POS, POS)
        return (q // (2 * Z), lax.rem(q // 2, Z), y, lax.rem(q, 2))

    far = chain_dev(pos + 2 * c - 1)
    right_dev, left_dev = chain_dev(pos + 1), chain_dev(pos - 1)

    stores = {}

    def store(*which):
        for name in which:
            stores[name] = pltpu.make_async_copy(
                getattr(R, name + "_b"), getattr(R, name + "_o"), R.out_s.at[len(stores)]
            )
            stores[name].start()

    loads = {}
    for i, (name, src) in enumerate(
        (("k", R.k_i), ("v", R.v_i), ("q", R.q_i), ("g", R.g_i), ("w", R.w_i.at[y]), ("gain", R.gain_i), ("bias", R.bias_i))
    ):
        loads[name] = pltpu.make_async_copy(src, getattr(R, name), R.in_s.at[i])
        loads[name].start()

    barrier = pltpu.get_barrier_semaphore()
    count = 0
    for o in range(1, N):
        pl.semaphore_signal(barrier, 1, device_id=inner_dev(lax.rem(n + o, N)), device_id_type=pl.DeviceIdType.MESH)
        count += 1
    for xo in range(1, X):
        for c2 in range(2):
            pl.semaphore_signal(
                barrier, 1, device_id=(lax.rem(x + xo, X), z, y, c2), device_id_type=pl.DeviceIdType.MESH
            )
            count += 1
    for o in range(1, Z):
        pl.semaphore_signal(barrier, 1, device_id=z_dev(o), device_id_type=pl.DeviceIdType.MESH)
        count += 1
    pl.semaphore_signal(barrier, 1, device_id=far, device_id_type=pl.DeviceIdType.MESH)
    count += 1

    loads["k"].wait()
    loads["v"].wait()
    for pair in range(Y // 2):
        R.kvm[2 * pair], R.kvm[2 * pair + 1] = pack_heads(R.k, R.v, pair)
    pl.semaphore_wait(barrier, count)

    unsent = []
    half = Y // 2
    core_in = y // half
    slot_in = lax.rem(y, half) * 2 + c
    self_in = c == core_in

    def send_in(src, dst, base, send, recv):
        for o in (*far_first(Y), 0):
            to = lax.rem(y + o, Y)
            remote = rcopy(src.at[to], dst.at[base + slot_in], send.at[o], recv.at[slot_in], (x, z, to, core_in))
            if o:
                remote.start()
                unsent.append(remote.wait_send)
            else:
                pl.when(jnp.logical_not(self_in))(remote.start)
                unsent.append(functools.partial(pl.when(jnp.logical_not(self_in)), remote.wait_send))

                @pl.when(self_in)
                def _():
                    pltpu.make_async_copy(src.at[y], dst.at[base + slot_in], recv.at[slot_in]).start()

    def received(src, dst, base, send, recv, j):
        rcopy(src.at[0], dst.at[base + j], send.at[0], recv.at[j], (x, z, y, c)).wait_recv()

    kv_move = (R.kvm, R.kvx, 1, R.kv_s, R.kv_r)
    qg_move = (R.qgm, R.qg, 0, R.qg_s, R.qg_r)
    send_in(*kv_move)
    loads["q"].wait()
    loads["g"].wait()
    for pair in range(Y // 2):
        R.qgm[2 * pair], R.qgm[2 * pair + 1] = pack_heads(R.q, R.g, pair)
    send_in(*qg_move)

    for name in ("w", "gain", "bias"):
        loads[name].wait()
    w_pad = jnp.concatenate([R.w[...], jnp.zeros((DH, LANDMARKS), BF16)], axis=0)
    R.wp[...] = w_pad
    R.wt[...] = w_pad.astype(F32).T.astype(BF16)
    gain = jnp.concatenate([R.gain[0:1, :], R.gain[1:2, :]], axis=1)
    bias = jnp.concatenate([R.bias[0:1, :], R.bias[1:2, :]], axis=1)

    for j in range(NS):
        received(*kv_move, j)

    kv_own = R.kvx[1 : NS + 1].reshape(NS * WIN, WIN)
    logits = mm_t(R.wt[...], kv_own)
    peak = jnp.max(logits, axis=1, keepdims=True)
    expo = jnp.exp(logits - peak)
    total = jnp.sum(expo, axis=1, keepdims=True)
    means = mm(expo.astype(BF16), kv_own) / total
    log_weights = peak + jnp.log(total)
    for p in range(G):
        rows = slice(p * CH, (p + 1) * CH)
        R.s1[p, 0:CH] = means[rows]
        R.s1[p, CH : CH + 8] = jnp.broadcast_to(as_row(log_weights[rows], 0), (8, WIN))

    def scatter_copies(src, dst, send, recv):
        return [
            rcopy(src.at[lax.rem(r + o, G)], dst.at[o - 1], send.at[o - 1], recv.at[o - 1], plane_dev(o))
            for o in far_first(G)
        ]

    def z_copies(src, dst, send, recv):
        return [rcopy(src, dst.at[o - 1], send.at[o - 1], recv.at[o - 1], z_dev(o)) for o in far_first(Z)]

    def gather_copies(buf, send, recv):
        return [
            rcopy(buf.at[r], buf.at[r], send.at[o - 1], recv.at[o - 1], plane_dev(o)) for o in far_first(G)
        ]

    def start(copies):
        for copy in copies:
            copy.start()
            unsent.append(copy.wait_send)
        return copies

    def arrive(copies):
        for copy in copies:
            copy.wait_recv()

    scatter_1 = start(scatter_copies(R.s1, R.r1, R.s1_s, R.s1_r))

    halo = start(
        [
            rcopy(R.kvx.at[NS], R.kvx.at[0], R.h_s.at[0], R.h_r.at[0], right_dev),
            rcopy(R.kvx.at[1], R.kvx.at[NS + 1], R.h_s.at[1], R.h_r.at[1], left_dev),
        ]
    )

    def transpose_kv(s):
        R.kvt[:, s * WIN : (s + 1) * WIN] = R.kvx[s].astype(F32).T.astype(BF16)

    for s in range(1, NS + 1):
        transpose_kv(s)

    def part_of(ref, o):
        return (ref[o, 0:CH], as_col(ref[o, CH : CH + 1], CH, 0))

    arrive(scatter_1)
    mean, log_weight = combine([part_of(R.s1, r)] + [part_of(R.r1, o) for o in range(G - 1)])
    R.s2[0:CH] = mean
    R.s2[CH : CH + 8] = jnp.broadcast_to(as_row(log_weight, 0), (8, WIN))
    z_1 = start(z_copies(R.s2, R.r2, R.s2_s, R.s2_r))

    arrive(halo)
    transpose_kv(0)
    transpose_kv(NS + 1)

    def window_scores(segs):
        for s in segs:
            received(*qg_move, s)
        for s in segs:
            qg = R.qg[s]
            left = left_half(qg.shape)
            zero = jnp.zeros_like(qg)
            R.rr[s, 0:WIN] = jnp.where(left, qg * jnp.asarray(0.125, BF16), zero)
            R.rr[s, WIN : 2 * WIN] = jnp.where(left, zero, qg)
        for s in segs:
            both = mm_t(R.kvx[s : s + 3].reshape(3 * WIN, WIN), R.rr[s])
            scores = both[:, 0:WIN]
            if s == 0:
                rows = lax.broadcasted_iota(jnp.int32, (3 * WIN, 1), 0)
                scores = scores + jnp.where((rows < WIN) & (pos == 0), -1e30, 0.0)
            if s == NS - 1:
                rows = lax.broadcasted_iota(jnp.int32, (3 * WIN, 1), 0)
                scores = scores + jnp.where((rows >= 2 * WIN) & (pos == POS - 1), -1e30, 0.0)
            R.sw[s] = scores
            R.gpw[s] = both[:, WIN:]
        tops = {s: jnp.max(R.sw[s], axis=0, keepdims=True) for s in segs}
        weights = {}
        for s in segs:
            weight = jnp.exp(R.sw[s] - tops[s])
            R.mw[s, 0:1] = tops[s]
            R.lw[s, 0:1] = jnp.sum(weight, axis=0, keepdims=True)
            R.dw[s, 0:1] = jnp.sum(weight * R.gpw[s], axis=0, keepdims=True)
            weights[s] = weight.astype(BF16)
        for s in segs:
            R.ow[s] = mm(R.kvt[:, s * WIN : (s + 3) * WIN], weights[s])

    split = (NS + 1) // 2
    window_scores(range(split))

    arrive(z_1)
    mean, log_weight = combine(
        [(mean, log_weight)] + [part_of(R.r2, o) for o in range(Z - 1)]
    )
    centred = mean - half_mean(mean)
    inverse = 1.0 / jnp.sqrt(half_mean(centred * centred) + 1e-05)
    normed = centred * inverse
    R.land[r] = (normed * gain + bias).astype(BF16)
    gather_1 = start(gather_copies(R.land, R.g1_s, R.g1_r))
    base = lax.rem(r * CH, WIN)
    R.lt[r] = jnp.broadcast_to(as_row(log_weight, base), (8, WIN))
    gather_l = start(gather_copies(R.lt, R.gl_s, R.gl_r))

    window_scores(range(split, NS))

    arrive(gather_1)

    land = R.land[...].reshape(LANDMARKS, WIN)
    every = range(NS)
    both = [mm_t(land, R.rr[s]) for s in every]
    tops = [jnp.maximum(R.mw[s, 0:1], jnp.max(both[s][:, 0:WIN], axis=0, keepdims=True)) for s in every]
    weights = [jnp.exp(both[s][:, 0:WIN] - tops[s]) for s in every]
    shrinks = [jnp.exp(R.mw[s, 0:1] - tops[s]) for s in every]
    totals = [R.lw[s, 0:1] * shrinks[s] + jnp.sum(weights[s], axis=0, keepdims=True) for s in every]
    pers = [1.0 / t for t in totals]
    probs = [w * per for w, per in zip(weights, pers)]
    deltas = [
        (R.dw[s, 0:1] * shrinks[s] + jnp.sum(weights[s] * both[s][:, WIN:], axis=0, keepdims=True)) * pers[s]
        for s in every
    ]
    for s in every:
        R.dp[:, (2 * s + 1) * WIN : (2 * s + 2) * WIN] = probs[s].astype(BF16)
        R.dp[:, 2 * s * WIN : (2 * s + 1) * WIN] = (probs[s] * (both[s][:, WIN:] - deltas[s])).astype(BF16)
    for s in every:
        R.mw[s, 0:1] = tops[s] + jnp.log(totals[s])
        R.lw[s, 0:1] = deltas[s]
        R.cf[s, 0:1] = shrinks[s] * pers[s]
    R.s3[...] = mm(R.dp[...], R.rr[...].reshape(2 * NS * WIN, WIN)).reshape(G, CH, WIN)
    scatter_2 = start(scatter_copies(R.s3, R.r3, R.s3_s, R.s3_r))

    R.dkv[...] = jnp.zeros_like(R.dkv)
    R.landt[...] = land.astype(F32).T.astype(BF16)

    def is_own(s):
        return n == c * NS + s

    def send_out(s, src, dst, send, recv):
        seg = c * NS + s
        copy = rcopy(src.at[s], dst.at[y], send.at[s], recv.at[y], (x, z, seg // 2, lax.rem(seg, 2)))
        pl.when(jnp.logical_not(is_own(s)))(copy.start)
        unsent.append(functools.partial(pl.when(jnp.logical_not(is_own(s))), copy.wait_send))

        @pl.when(is_own(s))
        def _():
            pltpu.make_async_copy(src.at[s], dst.at[y], recv.at[y]).start()

    def window_grads(segs):
        grads, probs_b = {}, {}
        for s in segs:
            probs = jnp.exp(R.sw[s] - R.mw[s, 0:1])
            grads[s] = (probs * (R.gpw[s] - R.lw[s, 0:1])).astype(BF16)
            probs_b[s] = probs.astype(BF16)
        for s in segs:
            part = mm(jnp.concatenate([grads[s], probs_b[s]], axis=1), R.rr[s])
            for i in range(3):
                R.dkv[s + i] += part[i * WIN : (i + 1) * WIN]
        rows = lax.broadcasted_iota(jnp.int32, (WIN, WIN), 0) < DH
        packed = []
        for s in segs:
            grad_q = mm(R.kvt[:, s * WIN : (s + 3) * WIN], grads[s]) + mm(
                R.landt[...], R.dp[:, 2 * s * WIN : (2 * s + 1) * WIN]
            )
            out_t = R.ow[s] * R.cf[s, 0:1] + mm(R.landt[...], R.dp[:, (2 * s + 1) * WIN : (2 * s + 2) * WIN])
            packed.append(jnp.where(rows, grad_q * 0.125, out_t))
        for s, block in zip(segs, packed):
            R.om[s] = block.T.astype(BF16)
        for s in segs:
            send_out(s, R.om, R.oi, R.o_s, R.o_r)

    window_grads(range(split))
    arrive(scatter_2)
    land_grad = R.s3[r]
    for o in range(G - 1):
        land_grad = land_grad + R.r3[o]
    R.s4[...] = land_grad
    z_2 = start(z_copies(R.s4, R.r4, R.s4_s, R.s4_r))
    window_grads(range(split, NS))
    back = start(
        [
            rcopy(R.dkv.at[NS + 1], R.dh.at[0], R.d_s.at[0], R.d_r.at[0], right_dev),
            rcopy(R.dkv.at[0], R.dh.at[1], R.d_s.at[1], R.d_r.at[1], left_dev),
        ]
    )
    arrive(z_2)
    for o in range(Z - 1):
        land_grad = land_grad + R.r4[o]
    scaled = land_grad * gain
    grad_mean = inverse * (scaled - half_mean(scaled) - normed * half_mean(scaled * normed))
    grad_mean_b = grad_mean.astype(BF16)
    R.gkv[r] = grad_mean_b
    gather_2 = start(gather_copies(R.gkv, R.g2_s, R.g2_r))
    column = jnp.sum(grad_mean_b.astype(F32) * mean, axis=1, keepdims=True)
    R.ct[r] = jnp.concatenate(
        [
            as_row(column, base),
            jnp.sum(land_grad * normed, axis=0, keepdims=True),
            jnp.sum(land_grad, axis=0, keepdims=True),
            jnp.zeros((5, WIN), F32),
        ],
        axis=0,
    )
    gather_c = start(gather_copies(R.ct, R.gc_s, R.gc_r))

    def row_of(ref):
        per = WIN // CH
        rows = []
        for first in range(0, G, per):
            rows.append(functools.reduce(lambda a, b: a + b, [ref[p, 0:1] for p in range(first, first + per)]))
        return jnp.concatenate(rows, axis=1)

    arrive(gather_l)
    log_row = row_of(R.lt)
    for s in range(NS):
        weight = jnp.exp(mm(R.kvx[s + 1], R.wp[...]) - log_row)
        R.wgt[s] = weight
        R.wgb[s] = weight.astype(BF16)
    arrive(back)
    R.dkv[1] += R.dh[0]
    R.dkv[NS] += R.dh[1]

    for h in range(Y):
        rcopy(R.om.at[0], R.oi.at[h], R.o_s.at[0], R.o_r.at[h], (x, z, y, c)).wait_recv()
    for pair in range(Y // 2):
        cols = slice(pair * WIN, (pair + 1) * WIN)
        R.gq_b[:, cols], R.att_b[:, cols] = unpack_heads(R.oi[2 * pair], R.oi[2 * pair + 1])
    store("gq", "att")

    arrive(gather_2)
    arrive(gather_c)
    column_row = row_of(R.ct)
    grads = R.gkv[...].reshape(LANDMARKS, WIN)
    for s in every:
        R.dl[s] = (R.wgt[s] * (mm_t(R.kvx[s + 1], grads) - column_row)).astype(BF16)
    R.nt[y] = functools.reduce(lambda a, b: a + b, [R.ct[p] for p in range(G)])
    norm_copies = start(
        [
            rcopy(R.nt.at[y], R.nt.at[y], R.n_s.at[o - 1], R.n_r.at[o - 1], (x, z, lax.rem(y + o, Y), c))
            for o in far_first(Y)
        ]
    )
    for first in range(0, NS, 4):
        segs = range(first, min(first + 4, NS))
        for s in segs:
            R.km[s] = (mm(R.wgb[s], grads) + mm(R.dl[s], R.wt[...]) + R.dkv[s + 1]).astype(BF16)
        for s in segs:
            send_out(s, R.km, R.ki, R.k_s, R.k_r)
    proj = mm(R.kvt[:, WIN : (NS + 1) * WIN], R.dl[...].reshape(NS * WIN, LANDMARKS)).T
    HN = LANDMARKS // N // 2
    halves = proj.reshape(N, 2, HN, WIN)
    low, high = halves[:, 0].reshape(N * HN, WIN), halves[:, 1].reshape(N * HN, WIN)
    R.pm[...] = jnp.where(left_half(low.shape), low, pltpu.roll(high, DH, 1)).reshape(N, HN, WIN)
    proj_copies = start(
        [
            rcopy(R.pm.at[lax.rem(n + o, N)], R.pi.at[n], R.p_s.at[o - 1], R.p_r.at[o - 1], inner_dev(lax.rem(n + o, N)))
            for o in far_first(N)
        ]
    )
    R.pi[n] = R.pm[n]
    for h in range(Y):
        rcopy(R.km.at[0], R.ki.at[h], R.k_s.at[0], R.k_r.at[h], (x, z, y, c)).wait_recv()
    for pair in range(Y // 2):
        cols = slice(pair * WIN, (pair + 1) * WIN)
        R.gk_b[:, cols], R.gv_b[:, cols] = unpack_heads(R.ki[2 * pair], R.ki[2 * pair + 1])
    store("gk", "gv")
    arrive(proj_copies)
    for h in range(Y):
        both = R.pi[2 * h] + R.pi[2 * h + 1]
        R.gp_b[h, 0:HN] = both[:, 0:DH]
        R.gp_b[h, HN : 2 * HN] = pltpu.roll(both, DH, 1)[:, 0:DH]
    arrive(norm_copies)
    sums = functools.reduce(lambda a, b: a + b, [R.nt[h] for h in range(Y)])
    R.gn_b[0:1] = sums[1:2, 0:DH]
    R.gn_b[1:2] = sums[2:3, 0:DH]
    R.gn_b[2:3] = sums[1:2, DH:]
    R.gn_b[3:4] = sums[2:3, DH:]

    store("gp", "gn")
    for wait in unsent:
        wait()
    for copy in stores.values():
        copy.wait()


def store_kernel(count, *refs):
    src, dst, via = (refs[i * count : (i + 1) * count] for i in range(3))
    read, written = refs[3 * count :]
    reads = [pltpu.make_async_copy(src[i], via[i], read.at[i]) for i in range(count)]
    writes = [pltpu.make_async_copy(via[i], dst[i], written.at[i]) for i in range(count)]
    for copy in reads:
        copy.start()
    for before, after in zip(reads, writes):
        before.wait()
        after.start()
    for copy in writes:
        copy.wait()


def layer(dims, q, k, v, w, gain, bias, g):
    X, Z, Y, C = dims
    NS, G, N = Y, 2 * X, 2 * Y
    CH, LN = LANDMARKS // G, LANDMARKS // N
    block = (WIN, WIN)
    dma = pltpu.SemaphoreType.DMA
    tokens = ((WIN, Y * DH), BF16)
    scratch = dict(
        q=tokens,
        k=tokens,
        v=tokens,
        g=tokens,
        w=((DH, LANDMARKS), BF16),
        gain=((2, DH), F32),
        bias=((2, DH), F32),
        kvm=((Y, *block), BF16),
        qgm=((Y, *block), BF16),
        kvx=((NS + 2, *block), BF16),
        qg=((NS, *block), BF16),
        wp=((WIN, LANDMARKS), BF16),
        wt=((LANDMARKS, WIN), BF16),
        s1=((G, CH + 8, WIN), F32),
        r1=((G - 1, CH + 8, WIN), F32),
        s2=((CH + 8, WIN), F32),
        r2=((Z - 1, CH + 8, WIN), F32),
        kvt=((WIN, (NS + 2) * WIN), BF16),
        rr=((NS, 2 * WIN, WIN), BF16),
        dw=((NS, 8, WIN), F32),
        cf=((NS, 8, WIN), F32),
        sw=((NS, 3 * WIN, WIN), F32),
        gpw=((NS, 3 * WIN, WIN), F32),
        mw=((NS, 8, WIN), F32),
        lw=((NS, 8, WIN), F32),
        ow=((NS, *block), F32),
        land=((G, CH, WIN), BF16),
        lt=((G, 8, WIN), F32),
        landt=((WIN, LANDMARKS), BF16),
        dp=((LANDMARKS, 2 * NS * WIN), BF16),
        s3=((G, CH, WIN), F32),
        r3=((G - 1, CH, WIN), F32),
        s4=((CH, WIN), F32),
        r4=((Z - 1, CH, WIN), F32),
        dkv=((NS + 2, *block), F32),
        dh=((2, *block), F32),
        om=((NS, *block), BF16),
        oi=((Y, *block), BF16),
        gkv=((G, CH, WIN), BF16),
        ct=((G, 8, WIN), F32),
        wgt=((NS, WIN, LANDMARKS), F32),
        wgb=((NS, WIN, LANDMARKS), BF16),
        dl=((NS, WIN, LANDMARKS), BF16),
        km=((NS, *block), BF16),
        ki=((Y, *block), BF16),
        pm=((N, LN // 2, WIN), F32),
        pi=((N, LN // 2, WIN), F32),
        nt=((Y, 8, WIN), F32),
    )
    counts = dict(
        kv=Y, qg=Y, h=2, s1=G - 1, s2=Z - 1, g1=G - 1, gl=G - 1, s3=G - 1, s4=Z - 1, g2=G - 1, gc=G - 1,
        d=2, o=Y, k=Y, p=N - 1, n=Y - 1,
    )
    sems = {f"{name}_{side}": dma((count,)) for name, count in counts.items() for side in "sr"}
    sems["in_s"] = dma((7,))
    outs = dict(
        att_o=tokens,
        gq_o=tokens,
        gk_o=tokens,
        gv_o=tokens,
        gp_o=((Y, LN, DH), F32),
        gn_o=((4, DH), F32),
    )
    scratch.update({name[:-2] + "_b": o for name, o in outs.items()})
    sems["out_s"] = dma((len(outs),))
    names = ("q_i", "k_i", "v_i", "w_i", "gain_i", "bias_i", "g_i", *outs, *scratch, *sems)
    results = pl.pallas_call(
        functools.partial(kernel, dims, names),
        out_shape=[jax.ShapeDtypeStruct(*o) for o in outs.values()],
        in_specs=[pl.BlockSpec(memory_space=pl.ANY)] * 7,
        out_specs=[pl.BlockSpec(memory_space=pl.ANY)] * len(outs),
        scratch_shapes=[pltpu.VMEM(*s) for s in scratch.values()] + list(sems.values()),
        compiler_params=pltpu.CompilerParams(
            collective_id=0, has_side_effects=True, vmem_limit_bytes=60 * 1024 * 1024
        ),
    )(q, k, v, w, gain, bias, g)
    att, gq, gk, gv, gp, gn = pl.pallas_call(
        functools.partial(store_kernel, len(outs)),
        out_shape=[jax.ShapeDtypeStruct(*o) for o in outs.values()],
        in_specs=[pl.BlockSpec(memory_space=pl.ANY)] * len(outs),
        out_specs=[pl.BlockSpec(memory_space=pl.ANY)] * len(outs),
        scratch_shapes=[pltpu.VMEM(*o) for o in outs.values()] + [dma((len(outs),))] * 2,
    )(*results)
    return att, gq, gk, gv, gp.transpose(0, 2, 1)[None], gn


def build(devices):
    finer = Mesh(devices, AXES)
    tokens = P(AXES, None)
    return jax.shard_map(
        functools.partial(layer, devices.shape),
        mesh=finer,
        in_specs=(tokens, tokens, tokens, P(), P(), P(), tokens),
        out_specs=(tokens, tokens, tokens, tokens, P(("x", "z"), None, None, ("y", "c")), P()),
        check_vma=False,
    )


def solution(mesh):
    return build(mesh.devices.reshape(4, 8, 8, 2))
```

```python
import functools
import types

import jax
import jax.numpy as jnp
from jax import lax
from jax.experimental import pallas as pl
from jax.experimental.pallas import tpu as pltpu
from jax.sharding import Mesh
from jax.sharding import PartitionSpec as P

AXES = ("x", "z", "y", "c")
WIN = 128
DH = 64
LANDMARKS = 256
F32 = jnp.float32
BF16 = jnp.bfloat16


def rcopy(src, dst, send, recv, device):
    return pltpu.make_async_remote_copy(
        src_ref=src,
        dst_ref=dst,
        send_sem=send,
        recv_sem=recv,
        device_id=device,
        device_id_type=pl.DeviceIdType.MESH,
    )


def mm(a, b):
    return lax.dot_general(a, b, (((1,), (0,)), ((), ())), preferred_element_type=F32)


def mm_t(a, b):
    return lax.dot_general(a, b, (((1,), (1,)), ((), ())), preferred_element_type=F32)


def far_first(size):
    return sorted(range(1, size), key=lambda o: -min(o, size - o))


def left_half(shape):
    return lax.broadcasted_iota(jnp.int32, shape, 1) < DH


def half_mean(x):
    left = left_half(x.shape)
    low = jnp.sum(jnp.where(left, x, 0.0), axis=1, keepdims=True)
    high = jnp.sum(jnp.where(left, 0.0, x), axis=1, keepdims=True)
    return jnp.where(left, low, high) * (1.0 / DH)


def pack_heads(a_ref, b_ref, pair):
    cols = pl.ds(pair * WIN, WIN)
    a, b = a_ref[:, cols].astype(F32), b_ref[:, cols].astype(F32)
    left = left_half(a.shape)
    even = jnp.where(left, a, pltpu.roll(b, DH, 1)).astype(BF16)
    odd = jnp.where(left, pltpu.roll(a, DH, 1), b).astype(BF16)
    return even, odd


def unpack_heads(even, odd):
    even, odd = even.astype(F32), odd.astype(F32)
    left = left_half(even.shape)
    a = jnp.where(left, even, pltpu.roll(odd, DH, 1)).astype(BF16)
    b = jnp.where(left, pltpu.roll(even, DH, 1), odd).astype(BF16)
    return a, b


def as_row(col, base):
    shape = (col.shape[0], WIN)
    diag = lax.broadcasted_iota(jnp.int32, shape, 1) == lax.broadcasted_iota(jnp.int32, shape, 0) + base
    return jnp.sum(jnp.where(diag, col, 0.0), axis=0, keepdims=True)


def as_col(row, n, base):
    shape = (n, WIN)
    diag = lax.broadcasted_iota(jnp.int32, shape, 1) == lax.broadcasted_iota(jnp.int32, shape, 0) + base
    return jnp.sum(jnp.where(diag, row, 0.0), axis=1, keepdims=True)


def split_row(row, rows):
    pieces = []
    rest = row
    for _ in range(3):
        pieces.append(rest.astype(BF16).astype(F32))
        rest = rest - pieces[-1]
    return jnp.concatenate([*pieces, jnp.zeros((rows - 3, row.shape[1]), F32)], axis=0).astype(BF16)


def join_rows(block):
    block = block.astype(F32)
    return block[0:1] + (block[1:2] + block[2:3])


def combine(parts, n):
    peak = functools.reduce(jnp.maximum, [row for _, row in parts])
    weights = [jnp.exp(row - peak) for _, row in parts]
    total = functools.reduce(lambda a, b: a + b, weights)
    per = 1.0 / total
    scaled = [mean.astype(F32) * as_col(w * per, n, 0) for (mean, _), w in zip(parts, weights)]
    return functools.reduce(lambda a, b: a + b, scaled), peak + jnp.log(total)


def kernel(dims, names, *refs):
    X, Z, Y, C = dims
    R = types.SimpleNamespace(**dict(zip(names, refs)))
    NS = Y
    G = 2 * X
    CH = LANDMARKS // G
    N = 2 * Y
    POS = X * Z * 2
    x, z, y, c = (lax.axis_index(a) for a in AXES)
    r = x * 2 + c
    n = y * 2 + c
    g = x * Z + z
    pos = g * 2 + c

    def inner_dev(m):
        return (x, z, m // 2, lax.rem(m, 2))

    def plane_dev(o):
        p = lax.rem(r + o, G)
        return (p // 2, z, y, lax.rem(p, 2))

    def z_dev(o):
        return (x, lax.rem(z + o, Z), y, c)

    def chain_dev(q):
        q = lax.rem(q + POS, POS)
        return (q // (2 * Z), lax.rem(q // 2, Z), y, lax.rem(q, 2))

    far = chain_dev(pos + 2 * c - 1)
    right_dev, left_dev = chain_dev(pos + 1), chain_dev(pos - 1)

    stores = {}

    def store(*which):
        for name in which:
            stores[name] = pltpu.make_async_copy(
                getattr(R, name + "_b"), getattr(R, name + "_o"), R.out_s.at[len(stores)]
            )
            stores[name].start()

    loads = {}
    for i, (name, src) in enumerate(
        (("k", R.k_i), ("v", R.v_i), ("q", R.q_i), ("g", R.g_i), ("w", R.w_i.at[y]), ("gain", R.gain_i), ("bias", R.bias_i))
    ):
        loads[name] = pltpu.make_async_copy(src, getattr(R, name), R.in_s.at[i])
        loads[name].start()

    barrier = pltpu.get_barrier_semaphore()
    count = 0
    for o in range(1, N):
        pl.semaphore_signal(barrier, 1, device_id=inner_dev(lax.rem(n + o, N)), device_id_type=pl.DeviceIdType.MESH)
        count += 1
    for xo in range(1, X):
        for c2 in range(2):
            pl.semaphore_signal(
                barrier, 1, device_id=(lax.rem(x + xo, X), z, y, c2), device_id_type=pl.DeviceIdType.MESH
            )
            count += 1
    for o in range(1, Z):
        pl.semaphore_signal(barrier, 1, device_id=z_dev(o), device_id_type=pl.DeviceIdType.MESH)
        count += 1
    pl.semaphore_signal(barrier, 1, device_id=far, device_id_type=pl.DeviceIdType.MESH)
    count += 1

    loads["k"].wait()
    loads["v"].wait()
    for pair in range(Y // 2):
        R.kvm[2 * pair], R.kvm[2 * pair + 1] = pack_heads(R.k, R.v, pair)
    pl.semaphore_wait(barrier, count)

    unsent = []
    half = Y // 2
    core_in = y // half
    slot_in = lax.rem(y, half) * 2 + c
    self_in = c == core_in

    def send_in(src, dst, base, send, recv):
        for o in (*far_first(Y), 0):
            to = lax.rem(y + o, Y)
            remote = rcopy(src.at[to], dst.at[base + slot_in], send.at[o], recv.at[slot_in], (x, z, to, core_in))
            if o:
                remote.start()
                unsent.append(remote.wait_send)
            else:
                pl.when(jnp.logical_not(self_in))(remote.start)
                unsent.append(functools.partial(pl.when(jnp.logical_not(self_in)), remote.wait_send))

                @pl.when(self_in)
                def _():
                    pltpu.make_async_copy(src.at[y], dst.at[base + slot_in], recv.at[slot_in]).start()

    def received(src, dst, base, send, recv, j):
        rcopy(src.at[0], dst.at[base + j], send.at[0], recv.at[j], (x, z, y, c)).wait_recv()

    kv_move = (R.kvm, R.kvx, 1, R.kv_s, R.kv_r)
    qg_move = (R.qgm, R.qg, 0, R.qg_s, R.qg_r)
    send_in(*kv_move)
    loads["q"].wait()
    loads["g"].wait()
    for pair in range(Y // 2):
        R.qgm[2 * pair], R.qgm[2 * pair + 1] = pack_heads(R.q, R.g, pair)
    send_in(*qg_move)

    for name in ("w", "gain", "bias"):
        loads[name].wait()
    w_pad = jnp.concatenate([R.w[...], jnp.zeros((DH, LANDMARKS), BF16)], axis=0)
    R.wp[...] = w_pad
    R.wt[...] = w_pad.astype(F32).T.astype(BF16)
    gain = jnp.concatenate([R.gain[0:1, :], R.gain[1:2, :]], axis=1)
    bias = jnp.concatenate([R.bias[0:1, :], R.bias[1:2, :]], axis=1)

    for j in range(NS):
        received(*kv_move, j)

    kv_own = R.kvx[1 : NS + 1].reshape(NS * WIN, WIN)
    logits = mm_t(R.wt[...], kv_own)
    peak = jnp.max(logits, axis=1, keepdims=True)
    expo = jnp.exp(logits - peak)
    total = jnp.sum(expo, axis=1, keepdims=True)
    means = mm(expo.astype(BF16), kv_own) / total
    log_weights = peak + jnp.log(total)
    for p in range(G):
        rows = slice(p * CH, (p + 1) * CH)
        R.s1[p, 0:CH] = means[rows].astype(BF16)
        R.s1[p, CH : CH + 16] = split_row(as_row(log_weights[rows], 0), 16)

    def scatter_copies(src, dst, send, recv):
        return [
            rcopy(src.at[lax.rem(r + o, G)], dst.at[o - 1], send.at[o - 1], recv.at[o - 1], plane_dev(o))
            for o in far_first(G)
        ]

    def z_copies(src, dst, send, recv):
        return [rcopy(src, dst.at[o - 1], send.at[o - 1], recv.at[o - 1], z_dev(o)) for o in far_first(Z)]

    def gather_copies(buf, send, recv):
        return [
            rcopy(buf.at[r], buf.at[r], send.at[o - 1], recv.at[o - 1], plane_dev(o)) for o in far_first(G)
        ]

    def start(copies):
        for copy in copies:
            copy.start()
            unsent.append(copy.wait_send)
        return copies

    def arrive(copies):
        for copy in copies:
            copy.wait_recv()

    scatter_1 = start(scatter_copies(R.s1, R.r1, R.s1_s, R.s1_r))

    halo = start(
        [
            rcopy(R.kvx.at[NS], R.kvx.at[0], R.h_s.at[0], R.h_r.at[0], right_dev),
            rcopy(R.kvx.at[1], R.kvx.at[NS + 1], R.h_s.at[1], R.h_r.at[1], left_dev),
        ]
    )

    def transpose_kv(s):
        R.kvt[:, s * WIN : (s + 1) * WIN] = R.kvx[s].astype(F32).T.astype(BF16)

    for s in range(1, NS + 1):
        transpose_kv(s)

    def part_of(ref, o):
        return (ref[o, 0:CH], join_rows(ref[o, CH : CH + 16]))

    arrive(scatter_1)
    mean, log_weight = combine([part_of(R.s1, r)] + [part_of(R.r1, o) for o in range(G - 1)], CH)
    R.s2[0:CH] = mean.astype(BF16)
    R.s2[CH : CH + 16] = split_row(log_weight, 16)
    z_1 = start(z_copies(R.s2, R.r2, R.s2_s, R.s2_r))

    arrive(halo)
    transpose_kv(0)
    transpose_kv(NS + 1)

    def window_scores(segs):
        for s in segs:
            received(*qg_move, s)
        for s in segs:
            qg = R.qg[s]
            left = left_half(qg.shape)
            zero = jnp.zeros_like(qg)
            R.rr[s, 0:WIN] = jnp.where(left, qg * jnp.asarray(0.125, BF16), zero)
            R.rr[s, WIN : 2 * WIN] = jnp.where(left, zero, qg)
        for s in segs:
            both = mm_t(R.kvx[s : s + 3].reshape(3 * WIN, WIN), R.rr[s])
            scores = both[:, 0:WIN]
            if s == 0:
                rows = lax.broadcasted_iota(jnp.int32, (3 * WIN, 1), 0)
                scores = scores + jnp.where((rows < WIN) & (pos == 0), -1e30, 0.0)
            if s == NS - 1:
                rows = lax.broadcasted_iota(jnp.int32, (3 * WIN, 1), 0)
                scores = scores + jnp.where((rows >= 2 * WIN) & (pos == POS - 1), -1e30, 0.0)
            R.sw[s] = scores
            R.gpw[s] = both[:, WIN:]
        tops = {s: jnp.max(R.sw[s], axis=0, keepdims=True) for s in segs}
        weights = {}
        for s in segs:
            weight = jnp.exp(R.sw[s] - tops[s])
            R.mw[s, 0:1] = tops[s]
            R.lw[s, 0:1] = jnp.sum(weight, axis=0, keepdims=True)
            R.dw[s, 0:1] = jnp.sum(weight * R.gpw[s], axis=0, keepdims=True)
            weights[s] = weight.astype(BF16)
        for s in segs:
            R.ow[s] = mm(R.kvt[:, s * WIN : (s + 3) * WIN], weights[s])

    split = (NS + 1) // 2
    window_scores(range(split))

    arrive(z_1)
    mean, log_weight = combine(
        [(R.s2[0:CH], log_weight)] + [part_of(R.r2, o) for o in range(Z - 1)], CH
    )
    centred = mean - half_mean(mean)
    inverse = 1.0 / jnp.sqrt(half_mean(centred * centred) + 1e-05)
    normed = centred * inverse
    R.land[r] = (normed * gain + bias).astype(BF16)
    gather_1 = start(gather_copies(R.land, R.g1_s, R.g1_r))
    base = lax.rem(r * CH, WIN)
    R.lt[r] = jnp.broadcast_to(as_row(as_col(log_weight, CH, 0), base), (8, WIN))
    gather_l = start(gather_copies(R.lt, R.gl_s, R.gl_r))

    window_scores(range(split, NS))

    arrive(gather_1)

    land = R.land[...].reshape(LANDMARKS, WIN)
    every = range(NS)
    both = [mm_t(land, R.rr[s]) for s in every]
    tops = [jnp.maximum(R.mw[s, 0:1], jnp.max(both[s][:, 0:WIN], axis=0, keepdims=True)) for s in every]
    weights = [jnp.exp(both[s][:, 0:WIN] - tops[s]) for s in every]
    shrinks = [jnp.exp(R.mw[s, 0:1] - tops[s]) for s in every]
    totals = [R.lw[s, 0:1] * shrinks[s] + jnp.sum(weights[s], axis=0, keepdims=True) for s in every]
    pers = [1.0 / t for t in totals]
    probs = [w * per for w, per in zip(weights, pers)]
    deltas = [
        (R.dw[s, 0:1] * shrinks[s] + jnp.sum(weights[s] * both[s][:, WIN:], axis=0, keepdims=True)) * pers[s]
        for s in every
    ]
    for s in every:
        R.dp[:, (2 * s + 1) * WIN : (2 * s + 2) * WIN] = probs[s].astype(BF16)
        R.dp[:, 2 * s * WIN : (2 * s + 1) * WIN] = (probs[s] * (both[s][:, WIN:] - deltas[s])).astype(BF16)
    for s in every:
        R.mw[s, 0:1] = tops[s] + jnp.log(totals[s])
        R.lw[s, 0:1] = deltas[s]
        R.cf[s, 0:1] = shrinks[s] * pers[s]
    R.s3[...] = mm(R.dp[...], R.rr[...].reshape(2 * NS * WIN, WIN)).astype(BF16).reshape(G, CH, WIN)
    scatter_2 = start(scatter_copies(R.s3, R.r3, R.s3_s, R.s3_r))

    R.dkv[...] = jnp.zeros_like(R.dkv)
    R.landt[...] = land.astype(F32).T.astype(BF16)

    def is_own(s):
        return n == c * NS + s

    def send_out(s, src, dst, send, recv):
        seg = c * NS + s
        copy = rcopy(src.at[s], dst.at[y], send.at[s], recv.at[y], (x, z, seg // 2, lax.rem(seg, 2)))
        pl.when(jnp.logical_not(is_own(s)))(copy.start)
        unsent.append(functools.partial(pl.when(jnp.logical_not(is_own(s))), copy.wait_send))

        @pl.when(is_own(s))
        def _():
            pltpu.make_async_copy(src.at[s], dst.at[y], recv.at[y]).start()

    def window_grads(segs):
        grads, probs_b = {}, {}
        for s in segs:
            probs = jnp.exp(R.sw[s] - R.mw[s, 0:1])
            grads[s] = (probs * (R.gpw[s] - R.lw[s, 0:1])).astype(BF16)
            probs_b[s] = probs.astype(BF16)
        for s in segs:
            part = mm(jnp.concatenate([grads[s], probs_b[s]], axis=1), R.rr[s])
            for i in range(3):
                R.dkv[s + i] += part[i * WIN : (i + 1) * WIN]
        rows = lax.broadcasted_iota(jnp.int32, (WIN, WIN), 0) < DH
        packed = []
        for s in segs:
            grad_q = mm(R.kvt[:, s * WIN : (s + 3) * WIN], grads[s]) + mm(
                R.landt[...], R.dp[:, 2 * s * WIN : (2 * s + 1) * WIN]
            )
            out_t = R.ow[s] * R.cf[s, 0:1] + mm(R.landt[...], R.dp[:, (2 * s + 1) * WIN : (2 * s + 2) * WIN])
            packed.append(jnp.where(rows, grad_q * 0.125, out_t))
        for s, block in zip(segs, packed):
            R.om[s] = block.T.astype(BF16)
        for s in segs:
            send_out(s, R.om, R.oi, R.o_s, R.o_r)

    window_grads(range(split))
    arrive(scatter_2)
    land_grad = R.s3[r].astype(F32)
    for o in range(G - 1):
        land_grad = land_grad + R.r3[o].astype(F32)
    R.s4[...] = land_grad.astype(BF16)
    z_2 = start(z_copies(R.s4, R.r4, R.s4_s, R.s4_r))
    window_grads(range(split, NS))
    back = start(
        [
            rcopy(R.dkv.at[NS + 1], R.dh.at[0], R.d_s.at[0], R.d_r.at[0], right_dev),
            rcopy(R.dkv.at[0], R.dh.at[1], R.d_s.at[1], R.d_r.at[1], left_dev),
        ]
    )
    arrive(z_2)
    land_grad = R.s4[...].astype(F32)
    for o in range(Z - 1):
        land_grad = land_grad + R.r4[o].astype(F32)
    scaled = land_grad * gain
    grad_mean = inverse * (scaled - half_mean(scaled) - normed * half_mean(scaled * normed))
    grad_mean_b = grad_mean.astype(BF16)
    column = jnp.sum(grad_mean_b.astype(F32) * mean, axis=1, keepdims=True)
    R.gkv[r, 0:CH] = grad_mean_b
    R.gkv[r, CH : CH + 16] = split_row(as_row(column, base), 16)
    gather_2 = start(gather_copies(R.gkv, R.g2_s, R.g2_r))
    R.ct[r] = jnp.concatenate(
        [
            jnp.sum(land_grad * normed, axis=0, keepdims=True),
            jnp.sum(land_grad, axis=0, keepdims=True),
            jnp.zeros((6, WIN), F32),
        ],
        axis=0,
    )
    gather_c = start(gather_copies(R.ct, R.gc_s, R.gc_r))

    def row_of(pieces):
        per = WIN // CH
        rows = [
            functools.reduce(lambda a, b: a + b, [pieces[p] for p in range(first, first + per)])
            for first in range(0, G, per)
        ]
        return jnp.concatenate(rows, axis=1)

    arrive(gather_l)
    log_row = row_of([R.lt[p, 0:1] for p in range(G)])
    for s in range(NS):
        weight = jnp.exp(mm(R.kvx[s + 1], R.wp[...]) - log_row)
        R.wgt[s] = weight
        R.wgb[s] = weight.astype(BF16)
    arrive(back)
    R.dkv[1] += R.dh[0]
    R.dkv[NS] += R.dh[1]

    for h in range(Y):
        rcopy(R.om.at[0], R.oi.at[h], R.o_s.at[0], R.o_r.at[h], (x, z, y, c)).wait_recv()
    for pair in range(Y // 2):
        cols = slice(pair * WIN, (pair + 1) * WIN)
        R.gq_b[:, cols], R.att_b[:, cols] = unpack_heads(R.oi[2 * pair], R.oi[2 * pair + 1])
    store("gq", "att")

    arrive(gather_2)
    column_row = row_of([join_rows(R.gkv[p, CH : CH + 16]) for p in range(G)])
    grads = R.gkv[:, 0:CH].reshape(LANDMARKS, WIN)
    for s in every:
        R.dl[s] = (R.wgt[s] * (mm_t(R.kvx[s + 1], grads) - column_row)).astype(BF16)

    turn = lax.rem(y, half) + jnp.where(core_in == c, 0, half // 2)
    segs = [2 * lax.rem(turn + o, half) + i for o in (*far_first(half), 0) for i in range(2)]

    def send_kv_grads(segs):
        for s in segs:
            R.km[s] = (mm(R.wgb[s], grads) + mm(R.dl[s], R.wt[...]) + R.dkv[s + 1]).astype(BF16)
        for s in segs:
            send_out(s, R.km, R.ki, R.k_s, R.k_r)

    send_kv_grads(segs[: NS // 2])
    arrive(gather_c)
    R.nt[y] = functools.reduce(lambda a, b: a + b, [R.ct[p] for p in range(G)])
    norm_copies = start(
        [
            rcopy(R.nt.at[y], R.nt.at[y], R.n_s.at[o - 1], R.n_r.at[o - 1], (x, z, lax.rem(y + o, Y), c))
            for o in far_first(Y)
        ]
    )
    proj = mm(R.kvt[:, WIN : (NS + 1) * WIN], R.dl[...].reshape(NS * WIN, LANDMARKS)).T
    HN = LANDMARKS // N // 2
    halves = proj.reshape(N, 2, HN, WIN)
    low, high = halves[:, 0].reshape(N * HN, WIN), halves[:, 1].reshape(N * HN, WIN)
    R.pm[...] = jnp.where(left_half(low.shape), low, pltpu.roll(high, DH, 1)).reshape(N, HN, WIN)
    proj_copies = start(
        [
            rcopy(R.pm.at[lax.rem(n + o, N)], R.pi.at[n], R.p_s.at[o - 1], R.p_r.at[o - 1], inner_dev(lax.rem(n + o, N)))
            for o in far_first(N)
        ]
    )
    R.pi[n] = R.pm[n]
    send_kv_grads(segs[NS // 2 :])
    for h in range(Y):
        rcopy(R.km.at[0], R.ki.at[h], R.k_s.at[0], R.k_r.at[h], (x, z, y, c)).wait_recv()
    for pair in range(Y // 2):
        cols = slice(pair * WIN, (pair + 1) * WIN)
        R.gk_b[:, cols], R.gv_b[:, cols] = unpack_heads(R.ki[2 * pair], R.ki[2 * pair + 1])
    store("gk", "gv")
    arrive(proj_copies)
    for h in range(Y):
        both = R.pi[2 * h] + R.pi[2 * h + 1]
        R.gp_b[h, 0:HN] = both[:, 0:DH]
        R.gp_b[h, HN : 2 * HN] = pltpu.roll(both, DH, 1)[:, 0:DH]
    arrive(norm_copies)
    sums = functools.reduce(lambda a, b: a + b, [R.nt[h] for h in range(Y)])
    R.gn_b[0:1] = sums[0:1, 0:DH]
    R.gn_b[1:2] = sums[1:2, 0:DH]
    R.gn_b[2:3] = sums[0:1, DH:]
    R.gn_b[3:4] = sums[1:2, DH:]

    store("gp", "gn")
    for wait in unsent:
        wait()
    for copy in stores.values():
        copy.wait()


def store_kernel(count, *refs):
    src, dst, via = (refs[i * count : (i + 1) * count] for i in range(3))
    read, written = refs[3 * count :]
    reads = [pltpu.make_async_copy(src[i], via[i], read.at[i]) for i in range(count)]
    writes = [pltpu.make_async_copy(via[i], dst[i], written.at[i]) for i in range(count)]
    for copy in reads:
        copy.start()
    for before, after in zip(reads, writes):
        before.wait()
        after.start()
    for copy in writes:
        copy.wait()


def layer(dims, q, k, v, w, gain, bias, g):
    X, Z, Y, C = dims
    NS, G, N = Y, 2 * X, 2 * Y
    CH, LN = LANDMARKS // G, LANDMARKS // N
    block = (WIN, WIN)
    dma = pltpu.SemaphoreType.DMA
    tokens = ((WIN, Y * DH), BF16)
    scratch = dict(
        q=tokens,
        k=tokens,
        v=tokens,
        g=tokens,
        w=((DH, LANDMARKS), BF16),
        gain=((2, DH), F32),
        bias=((2, DH), F32),
        kvm=((Y, *block), BF16),
        qgm=((Y, *block), BF16),
        kvx=((NS + 2, *block), BF16),
        qg=((NS, *block), BF16),
        wp=((WIN, LANDMARKS), BF16),
        wt=((LANDMARKS, WIN), BF16),
        s1=((G, CH + 16, WIN), BF16),
        r1=((G - 1, CH + 16, WIN), BF16),
        s2=((CH + 16, WIN), BF16),
        r2=((Z - 1, CH + 16, WIN), BF16),
        kvt=((WIN, (NS + 2) * WIN), BF16),
        rr=((NS, 2 * WIN, WIN), BF16),
        dw=((NS, 8, WIN), F32),
        cf=((NS, 8, WIN), F32),
        sw=((NS, 3 * WIN, WIN), F32),
        gpw=((NS, 3 * WIN, WIN), F32),
        mw=((NS, 8, WIN), F32),
        lw=((NS, 8, WIN), F32),
        ow=((NS, *block), F32),
        land=((G, CH, WIN), BF16),
        lt=((G, 8, WIN), F32),
        landt=((WIN, LANDMARKS), BF16),
        dp=((LANDMARKS, 2 * NS * WIN), BF16),
        s3=((G, CH, WIN), BF16),
        r3=((G - 1, CH, WIN), BF16),
        s4=((CH, WIN), BF16),
        r4=((Z - 1, CH, WIN), BF16),
        dkv=((NS + 2, *block), F32),
        dh=((2, *block), F32),
        om=((NS, *block), BF16),
        oi=((Y, *block), BF16),
        gkv=((G, CH + 16, WIN), BF16),
        ct=((G, 8, WIN), F32),
        wgt=((NS, WIN, LANDMARKS), F32),
        wgb=((NS, WIN, LANDMARKS), BF16),
        dl=((NS, WIN, LANDMARKS), BF16),
        km=((NS, *block), BF16),
        ki=((Y, *block), BF16),
        pm=((N, LN // 2, WIN), F32),
        pi=((N, LN // 2, WIN), F32),
        nt=((Y, 8, WIN), F32),
    )
    counts = dict(
        kv=Y, qg=Y, h=2, s1=G - 1, s2=Z - 1, g1=G - 1, gl=G - 1, s3=G - 1, s4=Z - 1, g2=G - 1, gc=G - 1,
        d=2, o=Y, k=Y, p=N - 1, n=Y - 1,
    )
    sems = {f"{name}_{side}": dma((count,)) for name, count in counts.items() for side in "sr"}
    sems["in_s"] = dma((7,))
    outs = dict(
        att_o=tokens,
        gq_o=tokens,
        gk_o=tokens,
        gv_o=tokens,
        gp_o=((Y, LN, DH), F32),
        gn_o=((4, DH), F32),
    )
    scratch.update({name[:-2] + "_b": o for name, o in outs.items()})
    sems["out_s"] = dma((len(outs),))
    names = ("q_i", "k_i", "v_i", "w_i", "gain_i", "bias_i", "g_i", *outs, *scratch, *sems)
    results = pl.pallas_call(
        functools.partial(kernel, dims, names),
        out_shape=[jax.ShapeDtypeStruct(*o) for o in outs.values()],
        in_specs=[pl.BlockSpec(memory_space=pl.ANY)] * 7,
        out_specs=[pl.BlockSpec(memory_space=pl.ANY)] * len(outs),
        scratch_shapes=[pltpu.VMEM(*s) for s in scratch.values()] + list(sems.values()),
        compiler_params=pltpu.CompilerParams(
            collective_id=0, has_side_effects=True, vmem_limit_bytes=60 * 1024 * 1024
        ),
    )(q, k, v, w, gain, bias, g)
    att, gq, gk, gv, gp, gn = pl.pallas_call(
        functools.partial(store_kernel, len(outs)),
        out_shape=[jax.ShapeDtypeStruct(*o) for o in outs.values()],
        in_specs=[pl.BlockSpec(memory_space=pl.ANY)] * len(outs),
        out_specs=[pl.BlockSpec(memory_space=pl.ANY)] * len(outs),
        scratch_shapes=[pltpu.VMEM(*o) for o in outs.values()] + [dma((len(outs),))] * 2,
    )(*results)
    return att, gq, gk, gv, gp.transpose(0, 2, 1)[None], gn


def build(devices):
    finer = Mesh(devices, AXES)
    tokens = P(AXES, None)
    return jax.shard_map(
        functools.partial(layer, devices.shape),
        mesh=finer,
        in_specs=(tokens, tokens, tokens, P(), P(), P(), tokens),
        out_specs=(tokens, tokens, tokens, tokens, P(("x", "z"), None, None, ("y", "c")), P()),
        check_vma=False,
    )


def solution(mesh):
    return build(mesh.devices.reshape(4, 8, 8, 2))
```

```python
import functools
import types

import jax
import jax.numpy as jnp
from jax import lax
from jax.experimental import pallas as pl
from jax.experimental.pallas import tpu as pltpu
from jax.sharding import Mesh
from jax.sharding import PartitionSpec as P

AXES = ("x", "z", "y", "c")
WIN = 128
DH = 64
LANDMARKS = 256
F32 = jnp.float32
BF16 = jnp.bfloat16


def rcopy(src, dst, send, recv, device):
    return pltpu.make_async_remote_copy(
        src_ref=src,
        dst_ref=dst,
        send_sem=send,
        recv_sem=recv,
        device_id=device,
        device_id_type=pl.DeviceIdType.MESH,
    )


def mm(a, b):
    return lax.dot_general(a, b, (((1,), (0,)), ((), ())), preferred_element_type=F32)


def mm_t(a, b):
    return lax.dot_general(a, b, (((1,), (1,)), ((), ())), preferred_element_type=F32)


def far_first(size):
    return sorted(range(1, size), key=lambda o: -min(o, size - o))


def left_half(shape):
    return lax.broadcasted_iota(jnp.int32, shape, 1) < DH


def half_mean(x):
    left = left_half(x.shape)
    low = jnp.sum(jnp.where(left, x, 0.0), axis=1, keepdims=True)
    high = jnp.sum(jnp.where(left, 0.0, x), axis=1, keepdims=True)
    return jnp.where(left, low, high) * (1.0 / DH)


def pack_heads(a_ref, b_ref, pair):
    cols = pl.ds(pair * WIN, WIN)
    a, b = a_ref[:, cols].astype(F32), b_ref[:, cols].astype(F32)
    left = left_half(a.shape)
    even = jnp.where(left, a, pltpu.roll(b, DH, 1)).astype(BF16)
    odd = jnp.where(left, pltpu.roll(a, DH, 1), b).astype(BF16)
    return even, odd


def unpack_heads(even, odd):
    even, odd = even.astype(F32), odd.astype(F32)
    left = left_half(even.shape)
    a = jnp.where(left, even, pltpu.roll(odd, DH, 1)).astype(BF16)
    b = jnp.where(left, pltpu.roll(even, DH, 1), odd).astype(BF16)
    return a, b


def as_row(col, base):
    shape = (col.shape[0], WIN)
    diag = lax.broadcasted_iota(jnp.int32, shape, 1) == lax.broadcasted_iota(jnp.int32, shape, 0) + base
    return jnp.sum(jnp.where(diag, col, 0.0), axis=0, keepdims=True)


def as_col(row, n, base):
    shape = (n, WIN)
    diag = lax.broadcasted_iota(jnp.int32, shape, 1) == lax.broadcasted_iota(jnp.int32, shape, 0) + base
    return jnp.sum(jnp.where(diag, row, 0.0), axis=1, keepdims=True)


def split_row(row, rows):
    pieces = []
    rest = row
    for _ in range(3):
        pieces.append(rest.astype(BF16).astype(F32))
        rest = rest - pieces[-1]
    return jnp.concatenate([*pieces, jnp.zeros((rows - 3, row.shape[1]), F32)], axis=0).astype(BF16)


def join_rows(block):
    block = block.astype(F32)
    return block[0:1] + (block[1:2] + block[2:3])


def combine(parts, n):
    peak = functools.reduce(jnp.maximum, [row for _, row in parts])
    weights = [jnp.exp(row - peak) for _, row in parts]
    total = functools.reduce(lambda a, b: a + b, weights)
    per = 1.0 / total
    scaled = [mean.astype(F32) * as_col(w * per, n, 0) for (mean, _), w in zip(parts, weights)]
    return functools.reduce(lambda a, b: a + b, scaled), peak + jnp.log(total)


def kernel(dims, names, *refs):
    X, Z, Y, C = dims
    R = types.SimpleNamespace(**dict(zip(names, refs)))
    NS = Y
    G = 2 * X
    CH = LANDMARKS // G
    N = 2 * Y
    POS = X * Z * 2
    x, z, y, c = (lax.axis_index(a) for a in AXES)
    r = x * 2 + c
    n = y * 2 + c
    g = x * Z + z
    pos = g * 2 + c

    def inner_dev(m):
        return (x, z, m // 2, lax.rem(m, 2))

    def plane_dev(o):
        p = lax.rem(r + o, G)
        return (p // 2, z, y, lax.rem(p, 2))

    def z_dev(o):
        return (x, lax.rem(z + o, Z), y, c)

    def chain_dev(q):
        q = lax.rem(q + POS, POS)
        return (q // (2 * Z), lax.rem(q // 2, Z), y, lax.rem(q, 2))

    far = chain_dev(pos + 2 * c - 1)
    right_dev, left_dev = chain_dev(pos + 1), chain_dev(pos - 1)

    stores = {}

    def store(*which):
        for name in which:
            stores[name] = pltpu.make_async_copy(
                getattr(R, name + "_b"), getattr(R, name + "_o"), R.out_s.at[len(stores)]
            )
            stores[name].start()

    loads = {}
    for i, (name, src) in enumerate(
        (("k", R.k_i), ("v", R.v_i), ("q", R.q_i), ("g", R.g_i), ("w", R.w_i.at[y]), ("gain", R.gain_i), ("bias", R.bias_i))
    ):
        loads[name] = pltpu.make_async_copy(src, getattr(R, name), R.in_s.at[i])
        loads[name].start()

    barrier = pltpu.get_barrier_semaphore()
    count = 0
    for o in range(1, N):
        pl.semaphore_signal(barrier, 1, device_id=inner_dev(lax.rem(n + o, N)), device_id_type=pl.DeviceIdType.MESH)
        count += 1
    for xo in range(1, X):
        for c2 in range(2):
            pl.semaphore_signal(
                barrier, 1, device_id=(lax.rem(x + xo, X), z, y, c2), device_id_type=pl.DeviceIdType.MESH
            )
            count += 1
    for o in range(1, Z):
        pl.semaphore_signal(barrier, 1, device_id=z_dev(o), device_id_type=pl.DeviceIdType.MESH)
        count += 1
    pl.semaphore_signal(barrier, 1, device_id=far, device_id_type=pl.DeviceIdType.MESH)
    count += 1

    loads["k"].wait()
    loads["v"].wait()
    for pair in range(Y // 2):
        R.kvm[2 * pair], R.kvm[2 * pair + 1] = pack_heads(R.k, R.v, pair)
    pl.semaphore_wait(barrier, count)

    unsent = []
    half = Y // 2
    core_in = y // half
    slot_in = lax.rem(y, half) * 2 + c
    self_in = c == core_in

    def send_in(src, dst, base, send, recv):
        for o in (*far_first(Y), 0):
            to = lax.rem(y + o, Y)
            remote = rcopy(src.at[to], dst.at[base + slot_in], send.at[o], recv.at[slot_in], (x, z, to, core_in))
            if o:
                remote.start()
                unsent.append(remote.wait_send)
            else:
                pl.when(jnp.logical_not(self_in))(remote.start)
                unsent.append(functools.partial(pl.when(jnp.logical_not(self_in)), remote.wait_send))

                @pl.when(self_in)
                def _():
                    pltpu.make_async_copy(src.at[y], dst.at[base + slot_in], recv.at[slot_in]).start()

    def received(src, dst, base, send, recv, j):
        rcopy(src.at[0], dst.at[base + j], send.at[0], recv.at[j], (x, z, y, c)).wait_recv()

    kv_move = (R.kvm, R.kvx, 1, R.kv_s, R.kv_r)
    qg_move = (R.qgm, R.qg, 0, R.qg_s, R.qg_r)
    send_in(*kv_move)
    loads["q"].wait()
    loads["g"].wait()
    for pair in range(Y // 2):
        R.qgm[2 * pair], R.qgm[2 * pair + 1] = pack_heads(R.q, R.g, pair)
    send_in(*qg_move)

    for name in ("w", "gain", "bias"):
        loads[name].wait()
    w_pad = jnp.concatenate([R.w[...], jnp.zeros((DH, LANDMARKS), BF16)], axis=0)
    R.wp[...] = w_pad
    R.wt[...] = w_pad.astype(F32).T.astype(BF16)
    gain = jnp.concatenate([R.gain[0:1, :], R.gain[1:2, :]], axis=1)
    bias = jnp.concatenate([R.bias[0:1, :], R.bias[1:2, :]], axis=1)

    for j in range(NS):
        received(*kv_move, j)

    def scatter_copies(src, dst, send, recv):
        return [
            rcopy(src.at[lax.rem(r + o, G)], dst.at[o - 1], send.at[o - 1], recv.at[o - 1], plane_dev(o))
            for o in far_first(G)
        ]

    def z_copies(src, dst, send, recv):
        return [rcopy(src, dst.at[o - 1], send.at[o - 1], recv.at[o - 1], z_dev(o)) for o in far_first(Z)]

    def gather_copies(buf, send, recv):
        return [
            rcopy(buf.at[r], buf.at[r], send.at[o - 1], recv.at[o - 1], plane_dev(o)) for o in far_first(G)
        ]

    def start(copies):
        for copy in copies:
            copy.start()
            unsent.append(copy.wait_send)
        return copies

    def arrive(copies):
        for copy in copies:
            copy.wait_recv()

    kv_own = R.kvx[1 : NS + 1].reshape(NS * WIN, WIN)
    R.lg[...] = mm_t(R.wt[...], kv_own).reshape(G, CH, NS * WIN)
    scatter_1 = scatter_copies(R.s1, R.r1, R.s1_s, R.s1_r)
    turns = (*far_first(G), 0)
    for first in range(0, G, G // 2):
        chunks = [lax.rem(r + o, G) for o in turns[first : first + G // 2]]
        peaks = [jnp.max(R.lg[p], axis=1, keepdims=True) for p in chunks]
        expos = [jnp.exp(R.lg[p] - peak) for p, peak in zip(chunks, peaks)]
        totals = [jnp.sum(expo, axis=1, keepdims=True) for expo in expos]
        sums = mm(jnp.concatenate([expo.astype(BF16) for expo in expos], axis=0), kv_own)
        for i, (p, peak, total) in enumerate(zip(chunks, peaks, totals)):
            R.s1[p, 0:CH] = (sums[i * CH : (i + 1) * CH] / total).astype(BF16)
            R.s1[p, CH : CH + 16] = split_row(as_row(peak + jnp.log(total), 0), 16)
        start(scatter_1[first : first + G // 2])


    halo = start(
        [
            rcopy(R.kvx.at[NS], R.kvx.at[0], R.h_s.at[0], R.h_r.at[0], right_dev),
            rcopy(R.kvx.at[1], R.kvx.at[NS + 1], R.h_s.at[1], R.h_r.at[1], left_dev),
        ]
    )

    def transpose_kv(s):
        R.kvt[:, s * WIN : (s + 1) * WIN] = R.kvx[s].astype(F32).T.astype(BF16)

    for s in range(1, NS + 1):
        transpose_kv(s)

    def part_of(ref, o):
        return (ref[o, 0:CH], join_rows(ref[o, CH : CH + 16]))

    arrive(scatter_1)
    mean, log_weight = combine([part_of(R.s1, r)] + [part_of(R.r1, o) for o in range(G - 1)], CH)
    R.s2[0:CH] = mean.astype(BF16)
    R.s2[CH : CH + 16] = split_row(log_weight, 16)
    z_1 = start(z_copies(R.s2, R.r2, R.s2_s, R.s2_r))

    arrive(halo)
    transpose_kv(0)
    transpose_kv(NS + 1)

    def window_scores(segs):
        for s in segs:
            received(*qg_move, s)
        for s in segs:
            qg = R.qg[s]
            left = left_half(qg.shape)
            zero = jnp.zeros_like(qg)
            R.rr[s, 0:WIN] = jnp.where(left, qg * jnp.asarray(0.125, BF16), zero)
            R.rr[s, WIN : 2 * WIN] = jnp.where(left, zero, qg)
        for s in segs:
            both = mm_t(R.kvx[s : s + 3].reshape(3 * WIN, WIN), R.rr[s])
            scores = both[:, 0:WIN]
            if s == 0:
                rows = lax.broadcasted_iota(jnp.int32, (3 * WIN, 1), 0)
                scores = scores + jnp.where((rows < WIN) & (pos == 0), -1e30, 0.0)
            if s == NS - 1:
                rows = lax.broadcasted_iota(jnp.int32, (3 * WIN, 1), 0)
                scores = scores + jnp.where((rows >= 2 * WIN) & (pos == POS - 1), -1e30, 0.0)
            R.sw[s] = scores
            R.gpw[s] = both[:, WIN:]
        tops = {s: jnp.max(R.sw[s], axis=0, keepdims=True) for s in segs}
        weights = {}
        for s in segs:
            weight = jnp.exp(R.sw[s] - tops[s])
            R.mw[s, 0:1] = tops[s]
            R.lw[s, 0:1] = jnp.sum(weight, axis=0, keepdims=True)
            R.dw[s, 0:1] = jnp.sum(weight * R.gpw[s], axis=0, keepdims=True)
            weights[s] = weight.astype(BF16)
        for s in segs:
            R.ow[s] = mm(R.kvt[:, s * WIN : (s + 3) * WIN], weights[s])

    split = (NS + 1) // 2
    window_scores(range(split))

    arrive(z_1)
    mean, log_weight = combine(
        [(R.s2[0:CH], log_weight)] + [part_of(R.r2, o) for o in range(Z - 1)], CH
    )
    centred = mean - half_mean(mean)
    inverse = 1.0 / jnp.sqrt(half_mean(centred * centred) + 1e-05)
    normed = centred * inverse
    R.land[r] = (normed * gain + bias).astype(BF16)
    gather_1 = start(gather_copies(R.land, R.g1_s, R.g1_r))
    base = lax.rem(r * CH, WIN)
    R.lt[r] = jnp.broadcast_to(as_row(as_col(log_weight, CH, 0), base), (8, WIN))
    gather_l = start(gather_copies(R.lt, R.gl_s, R.gl_r))

    window_scores(range(split, NS))

    arrive(gather_1)

    land = R.land[...].reshape(LANDMARKS, WIN)
    every = range(NS)
    both = [mm_t(land, R.rr[s]) for s in every]
    tops = [jnp.maximum(R.mw[s, 0:1], jnp.max(both[s][:, 0:WIN], axis=0, keepdims=True)) for s in every]
    weights = [jnp.exp(both[s][:, 0:WIN] - tops[s]) for s in every]
    shrinks = [jnp.exp(R.mw[s, 0:1] - tops[s]) for s in every]
    totals = [R.lw[s, 0:1] * shrinks[s] + jnp.sum(weights[s], axis=0, keepdims=True) for s in every]
    pers = [1.0 / t for t in totals]
    probs = [w * per for w, per in zip(weights, pers)]
    deltas = [
        (R.dw[s, 0:1] * shrinks[s] + jnp.sum(weights[s] * both[s][:, WIN:], axis=0, keepdims=True)) * pers[s]
        for s in every
    ]
    for s in every:
        R.dp[:, (2 * s + 1) * WIN : (2 * s + 2) * WIN] = probs[s].astype(BF16)
        R.dp[:, 2 * s * WIN : (2 * s + 1) * WIN] = (probs[s] * (both[s][:, WIN:] - deltas[s])).astype(BF16)
    for s in every:
        R.mw[s, 0:1] = tops[s] + jnp.log(totals[s])
        R.lw[s, 0:1] = deltas[s]
        R.cf[s, 0:1] = shrinks[s] * pers[s]
    R.s3[...] = mm(R.dp[...], R.rr[...].reshape(2 * NS * WIN, WIN)).astype(BF16).reshape(G, CH, WIN)
    scatter_2 = start(scatter_copies(R.s3, R.r3, R.s3_s, R.s3_r))

    R.dkv[...] = jnp.zeros_like(R.dkv)
    R.landt[...] = land.astype(F32).T.astype(BF16)

    def is_own(s):
        return n == c * NS + s

    def send_out(s, src, dst, send, recv):
        seg = c * NS + s
        copy = rcopy(src.at[s], dst.at[y], send.at[s], recv.at[y], (x, z, seg // 2, lax.rem(seg, 2)))
        pl.when(jnp.logical_not(is_own(s)))(copy.start)
        unsent.append(functools.partial(pl.when(jnp.logical_not(is_own(s))), copy.wait_send))

        @pl.when(is_own(s))
        def _():
            pltpu.make_async_copy(src.at[s], dst.at[y], recv.at[y]).start()

    def window_grads(segs):
        grads, probs_b = {}, {}
        for s in segs:
            probs = jnp.exp(R.sw[s] - R.mw[s, 0:1])
            grads[s] = (probs * (R.gpw[s] - R.lw[s, 0:1])).astype(BF16)
            probs_b[s] = probs.astype(BF16)
        for s in segs:
            part = mm(jnp.concatenate([grads[s], probs_b[s]], axis=1), R.rr[s])
            for i in range(3):
                R.dkv[s + i] += part[i * WIN : (i + 1) * WIN]
        rows = lax.broadcasted_iota(jnp.int32, (WIN, WIN), 0) < DH
        packed = []
        for s in segs:
            grad_q = mm(R.kvt[:, s * WIN : (s + 3) * WIN], grads[s]) + mm(
                R.landt[...], R.dp[:, 2 * s * WIN : (2 * s + 1) * WIN]
            )
            out_t = R.ow[s] * R.cf[s, 0:1] + mm(R.landt[...], R.dp[:, (2 * s + 1) * WIN : (2 * s + 2) * WIN])
            packed.append(jnp.where(rows, grad_q * 0.125, out_t))
        for s, block in zip(segs, packed):
            R.om[s] = block.T.astype(BF16)
        for s in segs:
            send_out(s, R.om, R.oi, R.o_s, R.o_r)

    window_grads(range(split))
    arrive(scatter_2)
    land_grad = R.s3[r].astype(F32)
    for o in range(G - 1):
        land_grad = land_grad + R.r3[o].astype(F32)
    R.s4[...] = land_grad.astype(BF16)
    z_2 = start(z_copies(R.s4, R.r4, R.s4_s, R.s4_r))
    window_grads(range(split, NS))
    back = start(
        [
            rcopy(R.dkv.at[NS + 1], R.dh.at[0], R.d_s.at[0], R.d_r.at[0], right_dev),
            rcopy(R.dkv.at[0], R.dh.at[1], R.d_s.at[1], R.d_r.at[1], left_dev),
        ]
    )
    arrive(z_2)
    land_grad = R.s4[...].astype(F32)
    for o in range(Z - 1):
        land_grad = land_grad + R.r4[o].astype(F32)
    scaled = land_grad * gain
    grad_mean = inverse * (scaled - half_mean(scaled) - normed * half_mean(scaled * normed))
    grad_mean_b = grad_mean.astype(BF16)
    column = jnp.sum(grad_mean_b.astype(F32) * mean, axis=1, keepdims=True)
    R.gkv[r, 0:CH] = grad_mean_b
    R.gkv[r, CH : CH + 16] = split_row(as_row(column, base), 16)
    gather_2 = start(gather_copies(R.gkv, R.g2_s, R.g2_r))
    R.ct[r] = jnp.concatenate(
        [
            jnp.sum(land_grad * normed, axis=0, keepdims=True),
            jnp.sum(land_grad, axis=0, keepdims=True),
            jnp.zeros((6, WIN), F32),
        ],
        axis=0,
    )
    gather_c = start(gather_copies(R.ct, R.gc_s, R.gc_r))

    def row_of(pieces):
        per = WIN // CH
        rows = [
            functools.reduce(lambda a, b: a + b, [pieces[p] for p in range(first, first + per)])
            for first in range(0, G, per)
        ]
        return jnp.concatenate(rows, axis=1)

    arrive(gather_l)
    log_row = row_of([R.lt[p, 0:1] for p in range(G)])
    for s in range(NS):
        weight = jnp.exp(mm(R.kvx[s + 1], R.wp[...]) - log_row)
        R.wgt[s] = weight
        R.wgb[s] = weight.astype(BF16)
    arrive(back)
    R.dkv[1] += R.dh[0]
    R.dkv[NS] += R.dh[1]

    for h in range(Y):
        rcopy(R.om.at[0], R.oi.at[h], R.o_s.at[0], R.o_r.at[h], (x, z, y, c)).wait_recv()
    for pair in range(Y // 2):
        cols = slice(pair * WIN, (pair + 1) * WIN)
        R.gq_b[:, cols], R.att_b[:, cols] = unpack_heads(R.oi[2 * pair], R.oi[2 * pair + 1])
    store("gq", "att")

    arrive(gather_2)
    column_row = row_of([join_rows(R.gkv[p, CH : CH + 16]) for p in range(G)])
    grads = R.gkv[:, 0:CH].reshape(LANDMARKS, WIN)
    turn = lax.rem(y, half) + jnp.where(core_in == c, 0, half // 2)
    segs = [2 * lax.rem(turn + o, half) + i for o in (*far_first(half), 0) for i in range(2)]

    def logit_grads(segs):
        for s in segs:
            R.dl[s] = (R.wgt[s] * (mm_t(R.kvx[s + 1], grads) - column_row)).astype(BF16)

    def send_kv_grads(segs):
        for s in segs:
            R.km[s] = (mm(R.wgb[s], grads) + mm(R.dl[s], R.wt[...]) + R.dkv[s + 1]).astype(BF16)
        for s in segs:
            send_out(s, R.km, R.ki, R.k_s, R.k_r)

    logit_grads(segs[: NS // 2])
    send_kv_grads(segs[: NS // 2])
    logit_grads(segs[NS // 2 :])
    arrive(gather_c)
    R.nm[...] = functools.reduce(lambda a, b: a + b, [R.ct[p] for p in range(G)])
    own_norm = pltpu.make_async_copy(R.nm, R.nt.at[y], R.own_s.at[1])
    own_norm.start()
    norm_copies = start(
        [
            rcopy(R.nm, R.nt.at[y], R.n_s.at[o - 1], R.n_r.at[o - 1], (x, z, lax.rem(y + o, Y), c))
            for o in far_first(Y)
        ]
    )
    proj = mm(R.kvt[:, WIN : (NS + 1) * WIN], R.dl[...].reshape(NS * WIN, LANDMARKS)).T
    HN = LANDMARKS // N // 2
    halves = proj.reshape(N, 2, HN, WIN)
    low, high = halves[:, 0].reshape(N * HN, WIN), halves[:, 1].reshape(N * HN, WIN)
    R.pm[...] = jnp.where(left_half(low.shape), low, pltpu.roll(high, DH, 1)).reshape(N, HN, WIN)
    proj_copies = start(
        [
            rcopy(R.pm.at[lax.rem(n + o, N)], R.pi.at[n], R.p_s.at[o - 1], R.p_r.at[o - 1], inner_dev(lax.rem(n + o, N)))
            for o in far_first(N)
        ]
    )
    own_proj = pltpu.make_async_copy(R.pm.at[n], R.pi.at[n], R.own_s.at[0])
    own_proj.start()
    send_kv_grads(segs[NS // 2 :])
    for h in range(Y):
        rcopy(R.km.at[0], R.ki.at[h], R.k_s.at[0], R.k_r.at[h], (x, z, y, c)).wait_recv()
    arrive(proj_copies)
    arrive(norm_copies)
    own_proj.wait()
    own_norm.wait()
    for wait in unsent:
        wait()
    for copy in stores.values():
        copy.wait()


def store_kernel(count, *refs):
    src = refs[:count]
    dst = refs[count : count + 6]
    got = refs[count + 6 : 2 * count + 6]
    via = refs[2 * count + 6 : 2 * count + 10]
    read, written = refs[-2:]
    reads = [pltpu.make_async_copy(src[i], got[i], read.at[i]) for i in range(count)]
    out = [got[0], got[1], *via]
    writes = [pltpu.make_async_copy(out[i], dst[i], written.at[i]) for i in range(6)]
    for copy in reads:
        copy.start()
    for i in range(2):
        reads[i].wait()
        writes[i].start()
    ki, pi, nt = got[2:]
    gk, gv, gp, gn = via
    reads[2].wait()
    for pair in range(ki.shape[0] // 2):
        cols = slice(pair * WIN, (pair + 1) * WIN)
        gk[:, cols], gv[:, cols] = unpack_heads(ki[2 * pair], ki[2 * pair + 1])
    writes[2].start()
    writes[3].start()
    reads[3].wait()
    half = pi.shape[1]
    for h in range(pi.shape[0] // 2):
        both = pi[2 * h] + pi[2 * h + 1]
        gp[h, 0:half] = both[:, 0:DH]
        gp[h, half : 2 * half] = pltpu.roll(both, DH, 1)[:, 0:DH]
    writes[4].start()
    reads[4].wait()
    sums = functools.reduce(lambda a, b: a + b, [nt[h] for h in range(nt.shape[0])])
    gn[0:1] = sums[0:1, 0:DH]
    gn[1:2] = sums[1:2, 0:DH]
    gn[2:3] = sums[0:1, DH:]
    gn[3:4] = sums[1:2, DH:]
    writes[5].start()
    for copy in writes:
        copy.wait()


def layer(dims, q, k, v, w, gain, bias, g):
    X, Z, Y, C = dims
    NS, G, N = Y, 2 * X, 2 * Y
    CH, LN = LANDMARKS // G, LANDMARKS // N
    block = (WIN, WIN)
    dma = pltpu.SemaphoreType.DMA
    tokens = ((WIN, Y * DH), BF16)
    scratch = dict(
        q=tokens,
        k=tokens,
        v=tokens,
        g=tokens,
        w=((DH, LANDMARKS), BF16),
        gain=((2, DH), F32),
        bias=((2, DH), F32),
        kvm=((Y, *block), BF16),
        qgm=((Y, *block), BF16),
        kvx=((NS + 2, *block), BF16),
        qg=((NS, *block), BF16),
        wp=((WIN, LANDMARKS), BF16),
        wt=((LANDMARKS, WIN), BF16),
        lg=((G, CH, NS * WIN), F32),
        s1=((G, CH + 16, WIN), BF16),
        r1=((G - 1, CH + 16, WIN), BF16),
        s2=((CH + 16, WIN), BF16),
        r2=((Z - 1, CH + 16, WIN), BF16),
        kvt=((WIN, (NS + 2) * WIN), BF16),
        rr=((NS, 2 * WIN, WIN), BF16),
        dw=((NS, 8, WIN), F32),
        cf=((NS, 8, WIN), F32),
        sw=((NS, 3 * WIN, WIN), F32),
        gpw=((NS, 3 * WIN, WIN), F32),
        mw=((NS, 8, WIN), F32),
        lw=((NS, 8, WIN), F32),
        ow=((NS, *block), F32),
        land=((G, CH, WIN), BF16),
        lt=((G, 8, WIN), F32),
        landt=((WIN, LANDMARKS), BF16),
        dp=((LANDMARKS, 2 * NS * WIN), BF16),
        s3=((G, CH, WIN), BF16),
        r3=((G - 1, CH, WIN), BF16),
        s4=((CH, WIN), BF16),
        r4=((Z - 1, CH, WIN), BF16),
        dkv=((NS + 2, *block), F32),
        dh=((2, *block), F32),
        om=((NS, *block), BF16),
        oi=((Y, *block), BF16),
        gkv=((G, CH + 16, WIN), BF16),
        ct=((G, 8, WIN), F32),
        wgt=((NS, WIN, LANDMARKS), F32),
        wgb=((NS, WIN, LANDMARKS), BF16),
        dl=((NS, WIN, LANDMARKS), BF16),
        km=((NS, *block), BF16),
        pm=((N, LN // 2, WIN), F32),
        nm=((8, WIN), F32),
    )
    counts = dict(
        kv=Y, qg=Y, h=2, s1=G - 1, s2=Z - 1, g1=G - 1, gl=G - 1, s3=G - 1, s4=Z - 1, g2=G - 1, gc=G - 1,
        d=2, o=Y, k=Y, p=N - 1, n=Y - 1,
    )
    sems = {f"{name}_{side}": dma((count,)) for name, count in counts.items() for side in "sr"}
    sems["in_s"] = dma((7,))
    sems["own_s"] = dma((2,))
    sems["out_s"] = dma((2,))
    sent = dict(
        att_o=tokens,
        gq_o=tokens,
        ki=((Y, *block), BF16),
        pi=((N, LN // 2, WIN), F32),
        nt=((Y, 8, WIN), F32),
    )
    scratch.update(att_b=tokens, gq_b=tokens)
    outs = [tokens, tokens, tokens, tokens, ((Y, LN, DH), F32), ((4, DH), F32)]
    names = ("q_i", "k_i", "v_i", "w_i", "gain_i", "bias_i", "g_i", *sent, *scratch, *sems)
    results = pl.pallas_call(
        functools.partial(kernel, dims, names),
        out_shape=[jax.ShapeDtypeStruct(*o) for o in sent.values()],
        in_specs=[pl.BlockSpec(memory_space=pl.ANY)] * 7,
        out_specs=[pl.BlockSpec(memory_space=pl.ANY)] * len(sent),
        scratch_shapes=[pltpu.VMEM(*s) for s in scratch.values()] + list(sems.values()),
        compiler_params=pltpu.CompilerParams(
            collective_id=0, has_side_effects=True, vmem_limit_bytes=60 * 1024 * 1024
        ),
    )(q, k, v, w, gain, bias, g)
    att, gq, gk, gv, gp, gn = pl.pallas_call(
        functools.partial(store_kernel, len(sent)),
        out_shape=[jax.ShapeDtypeStruct(*o) for o in outs],
        in_specs=[pl.BlockSpec(memory_space=pl.ANY)] * len(sent),
        out_specs=[pl.BlockSpec(memory_space=pl.ANY)] * len(outs),
        scratch_shapes=[pltpu.VMEM(*o) for o in (*sent.values(), *outs[2:])] + [dma((len(sent),)), dma((len(outs),))],
    )(*results)
    return att, gq, gk, gv, gp.transpose(0, 2, 1)[None], gn


def build(devices):
    finer = Mesh(devices, AXES)
    tokens = P(AXES, None)
    return jax.shard_map(
        functools.partial(layer, devices.shape),
        mesh=finer,
        in_specs=(tokens, tokens, tokens, P(), P(), P(), tokens),
        out_specs=(tokens, tokens, tokens, tokens, P(("x", "z"), None, None, ("y", "c")), P()),
        check_vma=False,
    )


def solution(mesh):
    return build(mesh.devices.reshape(4, 8, 8, 2))
```

```python
import functools
import types

import jax
import jax.numpy as jnp
from jax import lax
from jax.experimental import pallas as pl
from jax.experimental.pallas import tpu as pltpu
from jax.sharding import Mesh
from jax.sharding import PartitionSpec as P

AXES = ("x", "z", "y", "c")
WIN = 128
DH = 64
LANDMARKS = 256
F32 = jnp.float32
BF16 = jnp.bfloat16


def rcopy(src, dst, send, recv, device):
    return pltpu.make_async_remote_copy(
        src_ref=src,
        dst_ref=dst,
        send_sem=send,
        recv_sem=recv,
        device_id=device,
        device_id_type=pl.DeviceIdType.MESH,
    )


def mm(a, b):
    return lax.dot_general(a, b, (((1,), (0,)), ((), ())), preferred_element_type=F32)


def mm_t(a, b):
    return lax.dot_general(a, b, (((1,), (1,)), ((), ())), preferred_element_type=F32)


def far_first(size):
    return sorted(range(1, size), key=lambda o: -min(o, size - o))


def left_half(shape):
    return lax.broadcasted_iota(jnp.int32, shape, 1) < DH


def half_mean(x):
    left = left_half(x.shape)
    low = jnp.sum(jnp.where(left, x, 0.0), axis=1, keepdims=True)
    high = jnp.sum(jnp.where(left, 0.0, x), axis=1, keepdims=True)
    return jnp.where(left, low, high) * (1.0 / DH)


def pack_heads(a_ref, b_ref, pair):
    cols = pl.ds(pair * WIN, WIN)
    a, b = a_ref[:, cols].astype(F32), b_ref[:, cols].astype(F32)
    left = left_half(a.shape)
    even = jnp.where(left, a, pltpu.roll(b, DH, 1)).astype(BF16)
    odd = jnp.where(left, pltpu.roll(a, DH, 1), b).astype(BF16)
    return even, odd


def unpack_heads(even, odd):
    even, odd = even.astype(F32), odd.astype(F32)
    left = left_half(even.shape)
    a = jnp.where(left, even, pltpu.roll(odd, DH, 1)).astype(BF16)
    b = jnp.where(left, pltpu.roll(even, DH, 1), odd).astype(BF16)
    return a, b


def as_row(col, base):
    shape = (col.shape[0], WIN)
    diag = lax.broadcasted_iota(jnp.int32, shape, 1) == lax.broadcasted_iota(jnp.int32, shape, 0) + base
    return jnp.sum(jnp.where(diag, col, 0.0), axis=0, keepdims=True)


def as_col(row, n, base):
    shape = (n, WIN)
    diag = lax.broadcasted_iota(jnp.int32, shape, 1) == lax.broadcasted_iota(jnp.int32, shape, 0) + base
    return jnp.sum(jnp.where(diag, row, 0.0), axis=1, keepdims=True)


def split_row(row, rows):
    pieces = []
    rest = row
    for _ in range(3):
        pieces.append(rest.astype(BF16).astype(F32))
        rest = rest - pieces[-1]
    return jnp.concatenate([*pieces, jnp.zeros((rows - 3, row.shape[1]), F32)], axis=0).astype(BF16)


def join_rows(block):
    block = block.astype(F32)
    return block[0:1] + (block[1:2] + block[2:3])


def combine(parts, n):
    peak = functools.reduce(jnp.maximum, [row for _, row in parts])
    weights = [jnp.exp(row - peak) for _, row in parts]
    total = functools.reduce(lambda a, b: a + b, weights)
    per = 1.0 / total
    scaled = [mean.astype(F32) * as_col(w * per, n, 0) for (mean, _), w in zip(parts, weights)]
    return functools.reduce(lambda a, b: a + b, scaled), peak + jnp.log(total)


def kernel(dims, names, *refs):
    X, Z, Y, C = dims
    R = types.SimpleNamespace(**dict(zip(names, refs)))
    NS = Y
    G = 2 * X
    CH = LANDMARKS // G
    N = 2 * Y
    POS = X * Z * 2
    x, z, y, c = (lax.axis_index(a) for a in AXES)
    r = x * 2 + c
    n = y * 2 + c
    g = x * Z + z
    pos = g * 2 + c

    def inner_dev(m):
        return (x, z, m // 2, lax.rem(m, 2))

    def plane_dev(o):
        p = lax.rem(r + o, G)
        return (p // 2, z, y, lax.rem(p, 2))

    def z_dev(o):
        return (x, lax.rem(z + o, Z), y, c)

    def chain_dev(q):
        q = lax.rem(q + POS, POS)
        return (q // (2 * Z), lax.rem(q // 2, Z), y, lax.rem(q, 2))

    far = chain_dev(pos + 2 * c - 1)
    right_dev, left_dev = chain_dev(pos + 1), chain_dev(pos - 1)

    stores = {}

    def store(*which):
        for name in which:
            stores[name] = pltpu.make_async_copy(
                getattr(R, name + "_b"), getattr(R, name + "_o"), R.out_s.at[len(stores)]
            )
            stores[name].start()

    barrier = pltpu.get_barrier_semaphore()
    partners = [z_dev(o) for o in far_first(Z)]
    partners += [inner_dev(lax.rem(n + o, N)) for o in far_first(N)]
    partners += [(lax.rem(x + o, X), z, y, core) for o in far_first(X) for core in range(2)]
    partners.append(far)
    for partner in partners:
        pl.semaphore_signal(barrier, 1, device_id=partner, device_id_type=pl.DeviceIdType.MESH)
    count = len(partners)

    loads = {}
    for i, (name, src) in enumerate(
        (("k", R.k_i), ("v", R.v_i), ("q", R.q_i), ("g", R.g_i), ("w", R.w_i.at[y]), ("gain", R.gain_i), ("bias", R.bias_i))
    ):
        loads[name] = pltpu.make_async_copy(src, getattr(R, name), R.in_s.at[i])
        loads[name].start()

    loads["k"].wait()
    loads["v"].wait()
    for pair in range(Y // 2):
        R.kvm[2 * pair], R.kvm[2 * pair + 1] = pack_heads(R.k, R.v, pair)
    pl.semaphore_wait(barrier, count)

    unsent = []
    half = Y // 2
    core_in = y // half
    slot_in = lax.rem(y, half) * 2 + c
    self_in = c == core_in

    def send_in(src, dst, base, send, recv):
        for o in (*far_first(Y), 0):
            to = lax.rem(y + o, Y)
            remote = rcopy(src.at[to], dst.at[base + slot_in], send.at[o], recv.at[slot_in], (x, z, to, core_in))
            if o:
                remote.start()
                unsent.append(remote.wait_send)
            else:
                pl.when(jnp.logical_not(self_in))(remote.start)
                unsent.append(functools.partial(pl.when(jnp.logical_not(self_in)), remote.wait_send))

                @pl.when(self_in)
                def _():
                    pltpu.make_async_copy(src.at[y], dst.at[base + slot_in], recv.at[slot_in]).start()

    def received(src, dst, base, send, recv, j):
        rcopy(src.at[0], dst.at[base + j], send.at[0], recv.at[j], (x, z, y, c)).wait_recv()

    kv_move = (R.kvm, R.kvx, 1, R.kv_s, R.kv_r)
    qg_move = (R.qgm, R.qg, 0, R.qg_s, R.qg_r)
    send_in(*kv_move)
    loads["q"].wait()
    loads["g"].wait()
    for pair in range(Y // 2):
        R.qgm[2 * pair], R.qgm[2 * pair + 1] = pack_heads(R.q, R.g, pair)
    send_in(*qg_move)

    for name in ("w", "gain", "bias"):
        loads[name].wait()
    w_pad = jnp.concatenate([R.w[...], jnp.zeros((DH, LANDMARKS), BF16)], axis=0)
    R.wp[...] = w_pad
    R.wt[...] = w_pad.astype(F32).T.astype(BF16)
    gain = jnp.concatenate([R.gain[0:1, :], R.gain[1:2, :]], axis=1)
    bias = jnp.concatenate([R.bias[0:1, :], R.bias[1:2, :]], axis=1)

    for j in range(NS):
        received(*kv_move, j)

    def scatter_copies(src, dst, send, recv):
        return [
            rcopy(src.at[lax.rem(r + o, G)], dst.at[o - 1], send.at[o - 1], recv.at[o - 1], plane_dev(o))
            for o in far_first(G)
        ]

    def z_copies(src, dst, send, recv):
        return [rcopy(src, dst.at[o - 1], send.at[o - 1], recv.at[o - 1], z_dev(o)) for o in far_first(Z)]

    def gather_copies(buf, send, recv):
        return [
            rcopy(buf.at[r], buf.at[r], send.at[o - 1], recv.at[o - 1], plane_dev(o)) for o in far_first(G)
        ]

    def start(copies):
        for copy in copies:
            copy.start()
            unsent.append(copy.wait_send)
        return copies

    def arrive(copies):
        for copy in copies:
            copy.wait_recv()

    kv_own = R.kvx[1 : NS + 1].reshape(NS * WIN, WIN)
    R.lg[...] = mm_t(R.wt[...], kv_own).reshape(G, CH, NS * WIN)
    scatter_1 = scatter_copies(R.s1, R.r1, R.s1_s, R.s1_r)
    turns = (*far_first(G), 0)
    for first in range(0, G, G // 2):
        chunks = [lax.rem(r + o, G) for o in turns[first : first + G // 2]]
        peaks = [jnp.max(R.lg[p], axis=1, keepdims=True) for p in chunks]
        expos = [jnp.exp(R.lg[p] - peak) for p, peak in zip(chunks, peaks)]
        totals = [jnp.sum(expo, axis=1, keepdims=True) for expo in expos]
        sums = mm(jnp.concatenate([expo.astype(BF16) for expo in expos], axis=0), kv_own)
        for i, (p, peak, total) in enumerate(zip(chunks, peaks, totals)):
            R.s1[p, 0:CH] = (sums[i * CH : (i + 1) * CH] / total).astype(BF16)
            R.s1[p, CH : CH + 16] = split_row(as_row(peak + jnp.log(total), 0), 16)
        start(scatter_1[first : first + G // 2])


    halo = start(
        [
            rcopy(R.kvx.at[NS], R.kvx.at[0], R.h_s.at[0], R.h_r.at[0], right_dev),
            rcopy(R.kvx.at[1], R.kvx.at[NS + 1], R.h_s.at[1], R.h_r.at[1], left_dev),
        ]
    )

    def transpose_kv(s):
        R.kvt[:, s * WIN : (s + 1) * WIN] = R.kvx[s].astype(F32).T.astype(BF16)

    for s in range(1, NS + 1):
        transpose_kv(s)

    def part_of(ref, o):
        return (ref[o, 0:CH], join_rows(ref[o, CH : CH + 16]))

    arrive(scatter_1)
    mean, log_weight = combine([part_of(R.s1, r)] + [part_of(R.r1, o) for o in range(G - 1)], CH)
    R.s2[0:CH] = mean.astype(BF16)
    R.s2[CH : CH + 16] = split_row(log_weight, 16)
    z_1 = start(z_copies(R.s2, R.r2, R.s2_s, R.s2_r))

    arrive(halo)
    transpose_kv(0)
    transpose_kv(NS + 1)

    def window_scores(segs):
        for s in segs:
            received(*qg_move, s)
        for s in segs:
            qg = R.qg[s]
            left = left_half(qg.shape)
            zero = jnp.zeros_like(qg)
            R.rr[s, 0:WIN] = jnp.where(left, qg * jnp.asarray(0.125, BF16), zero)
            R.rr[s, WIN : 2 * WIN] = jnp.where(left, zero, qg)
        for s in segs:
            both = mm_t(R.kvx[s : s + 3].reshape(3 * WIN, WIN), R.rr[s])
            scores = both[:, 0:WIN]
            if s == 0:
                rows = lax.broadcasted_iota(jnp.int32, (3 * WIN, 1), 0)
                scores = scores + jnp.where((rows < WIN) & (pos == 0), -1e30, 0.0)
            if s == NS - 1:
                rows = lax.broadcasted_iota(jnp.int32, (3 * WIN, 1), 0)
                scores = scores + jnp.where((rows >= 2 * WIN) & (pos == POS - 1), -1e30, 0.0)
            R.sw[s] = scores
            R.gpw[s] = both[:, WIN:]
        tops = {s: jnp.max(R.sw[s], axis=0, keepdims=True) for s in segs}
        weights = {}
        for s in segs:
            weight = jnp.exp(R.sw[s] - tops[s])
            R.mw[s, 0:1] = tops[s]
            R.lw[s, 0:1] = jnp.sum(weight, axis=0, keepdims=True)
            R.dw[s, 0:1] = jnp.sum(weight * R.gpw[s], axis=0, keepdims=True)
            weights[s] = weight.astype(BF16)
        for s in segs:
            R.ow[s] = mm(R.kvt[:, s * WIN : (s + 3) * WIN], weights[s])

    split = (NS + 1) // 2
    window_scores(range(split))

    arrive(z_1)
    mean, log_weight = combine(
        [(R.s2[0:CH], log_weight)] + [part_of(R.r2, o) for o in range(Z - 1)], CH
    )
    centred = mean - half_mean(mean)
    inverse = 1.0 / jnp.sqrt(half_mean(centred * centred) + 1e-05)
    normed = centred * inverse
    R.land[r] = (normed * gain + bias).astype(BF16)
    gather_1 = start(gather_copies(R.land, R.g1_s, R.g1_r))
    base = lax.rem(r * CH, WIN)
    R.lt[r] = jnp.broadcast_to(as_row(as_col(log_weight, CH, 0), base), (8, WIN))
    gather_l = start(gather_copies(R.lt, R.gl_s, R.gl_r))

    window_scores(range(split, NS))

    arrive(gather_1)

    land = R.land[...].reshape(LANDMARKS, WIN)
    every = range(NS)
    both = [mm_t(land, R.rr[s]) for s in every]
    tops = [jnp.maximum(R.mw[s, 0:1], jnp.max(both[s][:, 0:WIN], axis=0, keepdims=True)) for s in every]
    weights = [jnp.exp(both[s][:, 0:WIN] - tops[s]) for s in every]
    shrinks = [jnp.exp(R.mw[s, 0:1] - tops[s]) for s in every]
    totals = [R.lw[s, 0:1] * shrinks[s] + jnp.sum(weights[s], axis=0, keepdims=True) for s in every]
    pers = [1.0 / t for t in totals]
    probs = [w * per for w, per in zip(weights, pers)]
    deltas = [
        (R.dw[s, 0:1] * shrinks[s] + jnp.sum(weights[s] * both[s][:, WIN:], axis=0, keepdims=True)) * pers[s]
        for s in every
    ]
    for s in every:
        R.dp[:, (2 * s + 1) * WIN : (2 * s + 2) * WIN] = probs[s].astype(BF16)
        R.dp[:, 2 * s * WIN : (2 * s + 1) * WIN] = (probs[s] * (both[s][:, WIN:] - deltas[s])).astype(BF16)
    for s in every:
        R.mw[s, 0:1] = tops[s] + jnp.log(totals[s])
        R.lw[s, 0:1] = deltas[s]
        R.cf[s, 0:1] = shrinks[s] * pers[s]
    R.s3[...] = mm(R.dp[...], R.rr[...].reshape(2 * NS * WIN, WIN)).astype(BF16).reshape(G, CH, WIN)
    scatter_2 = start(scatter_copies(R.s3, R.r3, R.s3_s, R.s3_r))

    R.dkv[...] = jnp.zeros_like(R.dkv)
    R.landt[...] = land.astype(F32).T.astype(BF16)

    def is_own(s):
        return n == c * NS + s

    def send_out(s, src, dst, send, recv):
        seg = c * NS + s
        copy = rcopy(src.at[s], dst.at[y], send.at[s], recv.at[y], (x, z, seg // 2, lax.rem(seg, 2)))
        pl.when(jnp.logical_not(is_own(s)))(copy.start)
        unsent.append(functools.partial(pl.when(jnp.logical_not(is_own(s))), copy.wait_send))

        @pl.when(is_own(s))
        def _():
            pltpu.make_async_copy(src.at[s], dst.at[y], recv.at[y]).start()

    def window_grads(segs):
        grads, probs_b = {}, {}
        for s in segs:
            probs = jnp.exp(R.sw[s] - R.mw[s, 0:1])
            grads[s] = (probs * (R.gpw[s] - R.lw[s, 0:1])).astype(BF16)
            probs_b[s] = probs.astype(BF16)
        for s in segs:
            part = mm(jnp.concatenate([grads[s], probs_b[s]], axis=1), R.rr[s])
            for i in range(3):
                R.dkv[s + i] += part[i * WIN : (i + 1) * WIN]
        rows = lax.broadcasted_iota(jnp.int32, (WIN, WIN), 0) < DH
        packed = []
        for s in segs:
            grad_q = mm(R.kvt[:, s * WIN : (s + 3) * WIN], grads[s]) + mm(
                R.landt[...], R.dp[:, 2 * s * WIN : (2 * s + 1) * WIN]
            )
            out_t = R.ow[s] * R.cf[s, 0:1] + mm(R.landt[...], R.dp[:, (2 * s + 1) * WIN : (2 * s + 2) * WIN])
            packed.append(jnp.where(rows, grad_q * 0.125, out_t))
        for s, block in zip(segs, packed):
            R.om[s] = block.T.astype(BF16)
        for s in segs:
            send_out(s, R.om, R.oi, R.o_s, R.o_r)

    window_grads(range(split))
    arrive(scatter_2)
    land_grad = R.s3[r].astype(F32)
    for o in range(G - 1):
        land_grad = land_grad + R.r3[o].astype(F32)
    R.s4[...] = land_grad.astype(BF16)
    z_2 = start(z_copies(R.s4, R.r4, R.s4_s, R.s4_r))
    window_grads(range(split, NS))
    back = start(
        [
            rcopy(R.dkv.at[NS + 1], R.dh.at[0], R.d_s.at[0], R.d_r.at[0], right_dev),
            rcopy(R.dkv.at[0], R.dh.at[1], R.d_s.at[1], R.d_r.at[1], left_dev),
        ]
    )
    arrive(z_2)
    land_grad = R.s4[...].astype(F32)
    for o in range(Z - 1):
        land_grad = land_grad + R.r4[o].astype(F32)
    scaled = land_grad * gain
    grad_mean = inverse * (scaled - half_mean(scaled) - normed * half_mean(scaled * normed))
    grad_mean_b = grad_mean.astype(BF16)
    column = jnp.sum(grad_mean_b.astype(F32) * mean, axis=1, keepdims=True)
    R.gkv[r, 0:CH] = grad_mean_b
    R.gkv[r, CH : CH + 16] = split_row(as_row(column, base), 16)
    gather_2 = start(gather_copies(R.gkv, R.g2_s, R.g2_r))
    R.ct[r] = jnp.concatenate(
        [
            jnp.sum(land_grad * normed, axis=0, keepdims=True),
            jnp.sum(land_grad, axis=0, keepdims=True),
            jnp.zeros((6, WIN), F32),
        ],
        axis=0,
    )
    gather_c = start(gather_copies(R.ct, R.gc_s, R.gc_r))

    def row_of(pieces):
        per = WIN // CH
        rows = [
            functools.reduce(lambda a, b: a + b, [pieces[p] for p in range(first, first + per)])
            for first in range(0, G, per)
        ]
        return jnp.concatenate(rows, axis=1)

    arrive(gather_l)
    log_row = row_of([R.lt[p, 0:1] for p in range(G)])
    for s in range(NS):
        weight = jnp.exp(mm(R.kvx[s + 1], R.wp[...]) - log_row)
        R.wgt[s] = weight
        R.wgb[s] = weight.astype(BF16)
    arrive(back)
    R.dkv[1] += R.dh[0]
    R.dkv[NS] += R.dh[1]

    for h in range(Y):
        rcopy(R.om.at[0], R.oi.at[h], R.o_s.at[0], R.o_r.at[h], (x, z, y, c)).wait_recv()
    for pair in range(Y // 2):
        cols = slice(pair * WIN, (pair + 1) * WIN)
        R.gq_b[:, cols], R.att_b[:, cols] = unpack_heads(R.oi[2 * pair], R.oi[2 * pair + 1])
    store("gq", "att")

    arrive(gather_2)
    column_row = row_of([join_rows(R.gkv[p, CH : CH + 16]) for p in range(G)])
    grads = R.gkv[:, 0:CH].reshape(LANDMARKS, WIN)
    turn = lax.rem(y, half) + jnp.where(core_in == c, 0, half // 2)
    segs = [2 * lax.rem(turn + o, half) + i for o in (*far_first(half), 0) for i in range(2)]

    def logit_grads(segs):
        for s in segs:
            R.dl[s] = (R.wgt[s] * (mm_t(R.kvx[s + 1], grads) - column_row)).astype(BF16)

    def send_kv_grads(segs):
        for s in segs:
            R.km[s] = (mm(R.wgb[s], grads) + mm(R.dl[s], R.wt[...]) + R.dkv[s + 1]).astype(BF16)
        for s in segs:
            send_out(s, R.km, R.ki, R.k_s, R.k_r)

    logit_grads(segs[: NS // 2])
    send_kv_grads(segs[: NS // 2])
    logit_grads(segs[NS // 2 :])
    arrive(gather_c)
    R.nm[...] = functools.reduce(lambda a, b: a + b, [R.ct[p] for p in range(G)])
    own_norm = pltpu.make_async_copy(R.nm, R.nt.at[y], R.own_s.at[1])
    own_norm.start()
    norm_copies = start(
        [
            rcopy(R.nm, R.nt.at[y], R.n_s.at[o - 1], R.n_r.at[o - 1], (x, z, lax.rem(y + o, Y), c))
            for o in far_first(Y)
        ]
    )
    proj = mm(R.kvt[:, WIN : (NS + 1) * WIN], R.dl[...].reshape(NS * WIN, LANDMARKS)).T
    HN = LANDMARKS // N // 2
    halves = proj.reshape(N, 2, HN, WIN)
    low, high = halves[:, 0].reshape(N * HN, WIN), halves[:, 1].reshape(N * HN, WIN)
    R.pm[...] = jnp.where(left_half(low.shape), low, pltpu.roll(high, DH, 1)).reshape(N, HN, WIN)
    proj_copies = start(
        [
            rcopy(R.pm.at[lax.rem(n + o, N)], R.pi.at[n], R.p_s.at[o - 1], R.p_r.at[o - 1], inner_dev(lax.rem(n + o, N)))
            for o in far_first(N)
        ]
    )
    own_proj = pltpu.make_async_copy(R.pm.at[n], R.pi.at[n], R.own_s.at[0])
    own_proj.start()
    send_kv_grads(segs[NS // 2 :])
    for h in range(Y):
        rcopy(R.km.at[0], R.ki.at[h], R.k_s.at[0], R.k_r.at[h], (x, z, y, c)).wait_recv()
    arrive(proj_copies)
    arrive(norm_copies)
    own_proj.wait()
    own_norm.wait()
    for wait in unsent:
        wait()
    for copy in stores.values():
        copy.wait()


def store_kernel(count, *refs):
    src = refs[:count]
    dst = refs[count : count + 6]
    got = refs[count + 6 : 2 * count + 6]
    via = refs[2 * count + 6 : 2 * count + 10]
    read, written = refs[-2:]
    reads = [pltpu.make_async_copy(src[i], got[i], read.at[i]) for i in range(count)]
    out = [got[0], got[1], *via]
    writes = [pltpu.make_async_copy(out[i], dst[i], written.at[i]) for i in range(6)]
    for copy in reads:
        copy.start()
    for i in range(2):
        reads[i].wait()
        writes[i].start()
    ki, pi, nt = got[2:]
    gk, gv, gp, gn = via
    reads[2].wait()
    for pair in range(ki.shape[0] // 2):
        cols = slice(pair * WIN, (pair + 1) * WIN)
        gk[:, cols], gv[:, cols] = unpack_heads(ki[2 * pair], ki[2 * pair + 1])
    writes[2].start()
    writes[3].start()
    reads[3].wait()
    half = pi.shape[1]
    for h in range(pi.shape[0] // 2):
        both = pi[2 * h] + pi[2 * h + 1]
        gp[h, 0:half] = both[:, 0:DH]
        gp[h, half : 2 * half] = pltpu.roll(both, DH, 1)[:, 0:DH]
    writes[4].start()
    reads[4].wait()
    sums = functools.reduce(lambda a, b: a + b, [nt[h] for h in range(nt.shape[0])])
    gn[0:1] = sums[0:1, 0:DH]
    gn[1:2] = sums[1:2, 0:DH]
    gn[2:3] = sums[0:1, DH:]
    gn[3:4] = sums[1:2, DH:]
    writes[5].start()
    for copy in writes:
        copy.wait()


def layer(dims, q, k, v, w, gain, bias, g):
    X, Z, Y, C = dims
    NS, G, N = Y, 2 * X, 2 * Y
    CH, LN = LANDMARKS // G, LANDMARKS // N
    block = (WIN, WIN)
    dma = pltpu.SemaphoreType.DMA
    tokens = ((WIN, Y * DH), BF16)
    scratch = dict(
        q=tokens,
        k=tokens,
        v=tokens,
        g=tokens,
        w=((DH, LANDMARKS), BF16),
        gain=((2, DH), F32),
        bias=((2, DH), F32),
        kvm=((Y, *block), BF16),
        qgm=((Y, *block), BF16),
        kvx=((NS + 2, *block), BF16),
        qg=((NS, *block), BF16),
        wp=((WIN, LANDMARKS), BF16),
        wt=((LANDMARKS, WIN), BF16),
        lg=((G, CH, NS * WIN), F32),
        s1=((G, CH + 16, WIN), BF16),
        r1=((G - 1, CH + 16, WIN), BF16),
        s2=((CH + 16, WIN), BF16),
        r2=((Z - 1, CH + 16, WIN), BF16),
        kvt=((WIN, (NS + 2) * WIN), BF16),
        rr=((NS, 2 * WIN, WIN), BF16),
        dw=((NS, 8, WIN), F32),
        cf=((NS, 8, WIN), F32),
        sw=((NS, 3 * WIN, WIN), F32),
        gpw=((NS, 3 * WIN, WIN), F32),
        mw=((NS, 8, WIN), F32),
        lw=((NS, 8, WIN), F32),
        ow=((NS, *block), F32),
        land=((G, CH, WIN), BF16),
        lt=((G, 8, WIN), F32),
        landt=((WIN, LANDMARKS), BF16),
        dp=((LANDMARKS, 2 * NS * WIN), BF16),
        s3=((G, CH, WIN), BF16),
        r3=((G - 1, CH, WIN), BF16),
        s4=((CH, WIN), BF16),
        r4=((Z - 1, CH, WIN), BF16),
        dkv=((NS + 2, *block), F32),
        dh=((2, *block), F32),
        om=((NS, *block), BF16),
        oi=((Y, *block), BF16),
        gkv=((G, CH + 16, WIN), BF16),
        ct=((G, 8, WIN), F32),
        wgt=((NS, WIN, LANDMARKS), F32),
        wgb=((NS, WIN, LANDMARKS), BF16),
        dl=((NS, WIN, LANDMARKS), BF16),
        km=((NS, *block), BF16),
        pm=((N, LN // 2, WIN), F32),
        nm=((8, WIN), F32),
    )
    counts = dict(
        kv=Y, qg=Y, h=2, s1=G - 1, s2=Z - 1, g1=G - 1, gl=G - 1, s3=G - 1, s4=Z - 1, g2=G - 1, gc=G - 1,
        d=2, o=Y, k=Y, p=N - 1, n=Y - 1,
    )
    sems = {f"{name}_{side}": dma((count,)) for name, count in counts.items() for side in "sr"}
    sems["in_s"] = dma((7,))
    sems["own_s"] = dma((2,))
    sems["out_s"] = dma((2,))
    sent = dict(
        att_o=tokens,
        gq_o=tokens,
        ki=((Y, *block), BF16),
        pi=((N, LN // 2, WIN), F32),
        nt=((Y, 8, WIN), F32),
    )
    scratch.update(att_b=tokens, gq_b=tokens)
    outs = [tokens, tokens, tokens, tokens, ((Y, LN, DH), F32), ((4, DH), F32)]
    names = ("q_i", "k_i", "v_i", "w_i", "gain_i", "bias_i", "g_i", *sent, *scratch, *sems)
    results = pl.pallas_call(
        functools.partial(kernel, dims, names),
        out_shape=[jax.ShapeDtypeStruct(*o) for o in sent.values()],
        in_specs=[pl.BlockSpec(memory_space=pl.ANY)] * 7,
        out_specs=[pl.BlockSpec(memory_space=pl.ANY)] * len(sent),
        scratch_shapes=[pltpu.VMEM(*s) for s in scratch.values()] + list(sems.values()),
        compiler_params=pltpu.CompilerParams(
            collective_id=0, has_side_effects=True, vmem_limit_bytes=60 * 1024 * 1024
        ),
    )(q, k, v, w, gain, bias, g)
    att, gq, gk, gv, gp, gn = pl.pallas_call(
        functools.partial(store_kernel, len(sent)),
        out_shape=[jax.ShapeDtypeStruct(*o) for o in outs],
        in_specs=[pl.BlockSpec(memory_space=pl.ANY)] * len(sent),
        out_specs=[pl.BlockSpec(memory_space=pl.ANY)] * len(outs),
        scratch_shapes=[pltpu.VMEM(*o) for o in (*sent.values(), *outs[2:])] + [dma((len(sent),)), dma((len(outs),))],
    )(*results)
    return att, gq, gk, gv, gp.transpose(0, 2, 1)[None], gn


def build(devices):
    finer = Mesh(devices, AXES)
    tokens = P(AXES, None)
    return jax.shard_map(
        functools.partial(layer, devices.shape),
        mesh=finer,
        in_specs=(tokens, tokens, tokens, P(), P(), P(), tokens),
        out_specs=(tokens, tokens, tokens, tokens, P(("x", "z"), None, None, ("y", "c")), P()),
        check_vma=False,
    )


def solution(mesh):
    return build(mesh.devices.reshape(4, 8, 8, 2))
```
